32 devices in a mesh: section: 2 (over y), dp: 4 (over x, core), tensor: 4 (over z).
Axes of the slice: x: 2, y: 2, z: 4, core: 2. Of those that a mesh axis runs over, the one named last changes fastest.
Arguments:
- inputs: bfloat16 [2, 1024, 12288], P('section', 'dp', 'tensor'), may hold values from -6 to 6
- queries: bfloat16 [2, 1024, 1024], P('section', 'dp', 'tensor'), may hold values from -8 to 8
- keys: bfloat16 [2, 1024, 1024], P('section', 'dp', 'tensor'), may hold values from -8 to 8
- w_value: bfloat16 [2, 12288, 1024], P('section', None, 'tensor'), may hold values from -0.0546875 to 0.0546875
- w_out: bfloat16 [2, 1024, 12288], P('section', 'tensor'), may hold values from -0.5 to 0.5
Outputs:
- next_inputs: bfloat16 [2, 1024, 12288], P('section', 'dp', 'tensor')
The draws below stay inside these ranges and needn't reach their ends.
All inputs are finite; a program needn't handle non-finite values.
Results may differ from the reference program's by a relative error of at most 0.023.
Values may be sent and summed in bfloat16 or wider, within the bound.
A program may use at most 64 MiB of HBM per device.

```python
import jax
import jax.numpy as jnp
from jax import lax

D = 12288
HEAD_SIZE = 128
HEAD_DEV = 2
LEN = 256
HEADS = 8
TOKENS = 1024
N_DP = 4
N_TENSOR = 4


def draw_queries(key, part):
    shape = (2, TOKENS, HEADS * HEAD_SIZE)
    return jnp.clip(jax.random.normal(jax.random.fold_in(key, 11), shape, jnp.float32), -4.0, 4.0).astype(jnp.bfloat16)


def draw_keys(key, part):
    shape = (2, TOKENS, HEADS * HEAD_SIZE)
    return jnp.clip(jax.random.normal(jax.random.fold_in(key, 13), shape, jnp.float32), -4.0, 4.0).astype(jnp.bfloat16)


def raised(entries, own_key, source, target, blocks, factor):
    owner, partner = [(jnp.arange(entries.shape[axis_at]) // (entries.shape[axis_at] // blocks)).reshape([-1 if axis == axis_at else 1 for axis in range(entries.ndim)]) for axis_at in (source, target)]
    chosen = jax.random.permutation(own_key, blocks)[partner]
    strong = (owner == chosen) | (owner == (partner + blocks // 2) % blocks)
    return jnp.where(strong, factor * entries, entries)


def block_scale(own_key, extent, shards, least, high):
    loudness, own = 1.0, jax.random.fold_in(own_key, 6)
    for dim, blocks in shards:
        heights = jnp.exp(jax.random.uniform(jax.random.fold_in(own, dim), (blocks,), jnp.float32, least / len(shards), high / len(shards)))
        loudness = loudness * jnp.repeat(heights, extent[dim] // blocks).reshape([-1 if axis == dim else 1 for axis in range(len(extent))])
    return loudness


def centred(key, extent, spread, bound, split=(), dtype=jnp.bfloat16):
    level = block_scale(key, extent, split, -0.22, 0.18) if split else 1.0
    values = jax.random.normal(key, extent, jnp.float32) * spread * level
    return jnp.minimum(jnp.maximum(values, -bound), bound).astype(dtype)


def gaussian_with(own_key, extent, width, reach, cuts, heavy, dtype=jnp.bfloat16):
    result = width * jax.random.normal(own_key, extent, jnp.float32)
    if cuts:
        result = result * block_scale(own_key, extent, cuts, -0.22, 0.18)
    return jnp.clip(raised(result, jax.random.fold_in(own_key, 3), *heavy), -reach, reach).astype(dtype)


def setup_inputs(seed: int = 0) -> dict:
    seeds = jax.random.split(jax.random.key(seed), 6)
    return {
        "inputs": centred(seeds[0], (2, TOKENS, D), 1.0, 6.0, ((0, 2), (1, 4), (2, 4))),
        "queries": draw_queries(jax.random.fold_in(seeds[5], 71), 0),
        "keys": draw_keys(jax.random.fold_in(seeds[5], 71), 0),
        "w_value": centred(seeds[3], (2, D, HEADS * HEAD_SIZE), D ** -0.5, 0.0546875, ((0, 2), (2, 4))),
        "w_out": gaussian_with(seeds[4], (2, HEADS * HEAD_SIZE, D), (HEAD_DEV * HEAD_SIZE) ** -0.5, 0.5, ((0, 2), (1, 4)), (1, 2, 4, 2.0)),
    }


def attend_one(parts):
    query_rows, key_rows, value_rows = parts
    scores = jnp.einsum('qhd,khd->hqk', query_rows.astype(jnp.float32), key_rows.astype(jnp.float32)) / jnp.sqrt(jnp.float32(HEAD_SIZE))
    rows = lax.broadcasted_iota(jnp.int32, (LEN, LEN), 0)
    cols = lax.broadcasted_iota(jnp.int32, (LEN, LEN), 1)
    scores = jnp.where((cols <= rows)[None], scores, jnp.float32(-1e+30))
    top = lax.optimization_barrier(jnp.max(scores, axis=-1, keepdims=True))
    expo = jnp.exp(scores - top)
    probs = (expo / lax.optimization_barrier(jnp.sum(expo, axis=-1, keepdims=True))).astype(jnp.bfloat16)
    return jnp.einsum('hqk,khd->qhd', probs.astype(jnp.float32), value_rows.astype(jnp.float32)).astype(jnp.bfloat16)

def block(activ, query_all, key_all, weight_v, weight_o):
    values = jnp.dot(activ, weight_v, preferred_element_type=jnp.float32).astype(jnp.bfloat16)
    shape4 = (N_DP, LEN, HEADS, HEAD_SIZE)
    context = lax.map(attend_one, (query_all.reshape(shape4), key_all.reshape(shape4), values.reshape(shape4)))
    group_dim = HEAD_DEV * HEAD_SIZE
    context = context.reshape(TOKENS, N_TENSOR, group_dim).transpose(1, 0, 2)
    weight_groups = weight_o.reshape(N_TENSOR, group_dim, D)

    def add_group(total, pair):
        term = jnp.dot(pair[0], pair[1], preferred_element_type=jnp.float32).astype(jnp.bfloat16)
        term = lax.optimization_barrier(term)
        return (total + term.astype(jnp.float32), None)
    total, unused = lax.scan(add_group, jnp.zeros((TOKENS, D), jnp.float32), (context, weight_groups))
    return (total + activ.astype(jnp.float32)).astype(jnp.bfloat16)

def reference(inputs, queries, keys, w_value, w_out):
    first = block(inputs[0], queries[0], keys[0], w_value[0], w_out[0])
    second = block(inputs[1], queries[1], keys[1], w_value[1], w_out[1])
    return jnp.stack([second, first])
```

```python
import functools

import jax
import jax.numpy as jnp
from jax import lax
from jax.experimental import pallas as pl
from jax.experimental.pallas import tpu as pltpu
from jax.sharding import PartitionSpec as P

HEAD_SIZE = 128
LEN = 256
V_SUB = 2
O_SUB = 2
WINDOW = 3
ORDER = (2, 1, 3)


def flip(index, bit):
    step = 2**bit
    return index + step - 2 * step * lax.rem(index // step, 2)


def flip_by(index, mask):
    for bit in range(mask.bit_length()):
        if mask >> bit & 1:
            index = flip(index, bit)
    return index


def moving_weights(
    n,
    activ_hbm, query_hbm, key_hbm, wv_hbm, wo_hbm, out_hbm,
    activ, query, key, wv, wo, part_out, part_in, context, result,
    local_sem, wv_send, wv_recv, wo_send, wo_recv, small_send, small_recv, out_send, out_recv,
):
    section = lax.axis_index("section")
    dp = lax.axis_index("dp")
    z = lax.axis_index("tensor")
    length, cols = activ.shape
    quarter = cols // 4
    v_rows = quarter // V_SUB
    o_cols = quarter // O_SUB
    core_peer = flip(dp, 0)
    chip_peer = flip(dp, 1)
    diagonal = flip(core_peer, 1)
    quarters = (dp, core_peer, chip_peer, diagonal)
    other = flip(section, 0)

    barrier = pltpu.get_barrier_semaphore()
    for slot in range(1, n):
        pl.semaphore_signal(barrier, inc=1, device_id=(section, dp, flip_by(z, slot)),
                            device_id_type=pl.DeviceIdType.MESH)
    for target in ((section, core_peer, z), (section, chip_peer, z), (other, dp, z)):
        pl.semaphore_signal(barrier, inc=1, device_id=target, device_id_type=pl.DeviceIdType.MESH)

    def remote(src, dst, send, recv, target):
        return pltpu.make_async_remote_copy(
            src_ref=src, dst_ref=dst, send_sem=send, recv_sem=recv,
            device_id=target, device_id_type=pl.DeviceIdType.MESH)

    own = pl.multiple_of(z * cols, cols)
    locals_ = [
        pltpu.make_async_copy(activ_hbm.at[0], activ, local_sem.at[0]),
        pltpu.make_async_copy(query_hbm.at[0], query, local_sem.at[1]),
        pltpu.make_async_copy(key_hbm.at[0], key, local_sem.at[2]),
        pltpu.make_async_copy(wv_hbm.at[0, pl.ds(own, cols), :], wv.at[0], local_sem.at[3]),
        pltpu.make_async_copy(wo_hbm.at[0, :, pl.ds(own, cols)], wo.at[0], local_sem.at[4]),
    ]
    pl.semaphore_wait(barrier, n + 2)

    pieces = [("v", slot, sub) for sub in range(V_SUB) for slot in ORDER]
    n_value = len(pieces)
    pieces += [("o", slot, sub) for sub in range(O_SUB) for slot in ORDER]

    def v_at(slot, which, sub):
        rows = pl.ds(pl.multiple_of(which * quarter + sub * v_rows, v_rows), v_rows)
        return wv.at[slot, rows, :]

    def o_at(slot, which, sub):
        columns = pl.ds(pl.multiple_of(which * quarter + sub * o_cols, o_cols), o_cols)
        return wo.at[slot, :, columns]

    def copies(piece):
        kind, slot, sub = piece
        peer = flip_by(z, slot)
        if kind == "v":
            start = pl.multiple_of(peer * cols + dp * quarter + sub * v_rows, v_rows)
            source = wv_hbm.at[0, pl.ds(start, v_rows), :]
            at, send, recv = v_at, wv_send, wv_recv
        else:
            start = pl.multiple_of(peer * cols + dp * quarter + sub * o_cols, o_cols)
            source = wo_hbm.at[0, :, pl.ds(start, o_cols)]
            at, send, recv = o_at, wo_send, wo_recv
        mine, far = at(slot, dp, sub), at(slot, chip_peer, sub)
        def sems(hop):
            return send.at[slot - 1, sub, hop], recv.at[slot - 1, sub, hop]
        return (
            remote(source, mine, *sems(0), (section, dp, peer)),
            remote(mine, mine, *sems(1), (section, core_peer, z)),
            remote(mine, mine, *sems(2), (section, chip_peer, z)),
            remote(far, far, *sems(3), (section, core_peer, z)),
        )

    plan = [copies(piece) for piece in pieces]
    for i in range(WINDOW):
        plan[i][0].start()
    for copy in locals_:
        copy.start()

    def step(i):
        plan[i][0].wait_recv()
        plan[i][2].start()
        plan[i][1].start()
        if i + WINDOW < len(plan):
            plan[i][0].wait_send()
            plan[i + WINDOW][0].start()
        if i > 0:
            relay(i - 1)

    def relay(i):
        plan[i][2].wait_recv()
        plan[i][3].start()

    def arrived(i):
        plan[i][1].wait_recv()
        plan[i][3].wait_recv()

    for i in range(n_value):
        step(i)
    relay(n_value - 1)
    for i in range(n_value):
        arrived(i)
    locals_[0].wait()
    locals_[3].wait()

    value_sends = []
    for slot in ORDER + (0,):
        term = jnp.dot(activ[...], wv[slot], preferred_element_type=jnp.float32)
        if slot == 0:
            mine_term = term
        else:
            part_out[slot - 1] = term.astype(jnp.bfloat16)
            copy = remote(part_out.at[slot - 1], part_in.at[slot - 1], small_send.at[0, slot - 1],
                          small_recv.at[0, slot - 1], (section, dp, flip_by(z, slot)))
            copy.start()
            value_sends.append(copy)
    locals_[1].wait()
    locals_[2].wait()

    total = mine_term
    for copy in value_sends:
        copy.wait_recv()
    for slot in range(1, n):
        total = total + part_in[slot - 1].astype(jnp.float32)
    values = total.astype(jnp.bfloat16)

    causal = lax.broadcasted_iota(jnp.int32, (LEN, LEN), 1) <= lax.broadcasted_iota(jnp.int32, (LEN, LEN), 0)
    scale = 1.0 / HEAD_SIZE**0.5
    for start in range(0, length, LEN):
        for head in range(0, query.shape[1], HEAD_SIZE):
            rows, span = slice(start, start + LEN), slice(head, head + HEAD_SIZE)
            scores = lax.dot_general(query[rows, span], key[rows, span], (((1,), (1,)), ((), ())),
                                     preferred_element_type=jnp.float32) * scale
            scores = jnp.where(causal, scores, -1e30)
            expo = jnp.exp(scores - jnp.max(scores, axis=-1, keepdims=True))
            probs = (expo / jnp.sum(expo, axis=-1, keepdims=True)).astype(jnp.bfloat16)
            context[0, rows, span] = jnp.dot(
                probs, values[rows, span], preferred_element_type=jnp.float32).astype(jnp.bfloat16)

    context_sends = []
    for slot in ORDER:
        copy = remote(context.at[0], context.at[slot], small_send.at[1, slot - 1],
                      small_recv.at[1, slot - 1], (section, dp, flip_by(z, slot)))
        copy.start()
        context_sends.append(copy)

    locals_[4].wait()
    out_sends = []
    per_sub = n - 1
    done = n_value
    for sub in range(O_SUB):
        for i in range(done, done + per_sub):
            plan_first = i == n_value
            plan[i][0].wait_recv()
            plan[i][2].start()
            plan[i][1].start()
            if i + WINDOW < len(plan):
                plan[i][0].wait_send()
                plan[i + WINDOW][0].start()
            if not plan_first:
                if i > done:
                    relay(i - 1)
        relay(done + per_sub - 1)
        if sub == 0:
            for copy in context_sends:
                copy.wait_recv()
        for order, which in enumerate(quarters):
            for i in range(done, done + per_sub):
                if order == 1:
                    plan[i][1].wait_recv()
                elif order == 3:
                    plan[i][3].wait_recv()
            start = pl.multiple_of(which * quarter + sub * o_cols, o_cols)
            columns = pl.ds(start, o_cols)
            total = activ[:, columns].astype(jnp.float32)
            for slot in range(n):
                total = total + jnp.dot(context[slot], wo[slot, :, columns],
                                        preferred_element_type=jnp.float32)
            result[sub * 4 + order] = total.astype(jnp.bfloat16)
            copy = remote(result.at[sub * 4 + order], out_hbm.at[0, :, columns],
                          out_send.at[sub * 4 + order], out_recv.at[sub * 4 + order], (other, dp, z))
            copy.start()
            out_sends.append(copy)
        done += per_sub

    for i, piece in enumerate(plan):
        if i + WINDOW >= len(plan):
            piece[0].wait_send()
        for copy in piece[1:]:
            copy.wait_send()
    for copy in value_sends + context_sends:
        copy.wait_send()
    for copy in out_sends:
        copy.wait()


def by_weights(n, inputs, queries, keys, w_value, w_out):
    length, cols = inputs.shape[1:]
    width = w_value.shape[2]
    bf16, dma = jnp.bfloat16, pltpu.SemaphoreType.DMA
    chunks = 4 * O_SUB
    return pl.pallas_call(
        functools.partial(moving_weights, n),
        out_shape=jax.ShapeDtypeStruct(inputs.shape, bf16),
        in_specs=[pl.BlockSpec(memory_space=pl.ANY)] * 5,
        out_specs=pl.BlockSpec(memory_space=pl.ANY),
        scratch_shapes=[
            pltpu.VMEM((length, cols), bf16),
            pltpu.VMEM((length, width), bf16),
            pltpu.VMEM((length, width), bf16),
            pltpu.VMEM((n, cols, width), bf16),
            pltpu.VMEM((n, width, cols), bf16),
            pltpu.VMEM((n - 1, length, width), bf16),
            pltpu.VMEM((n - 1, length, width), bf16),
            pltpu.VMEM((n, length, width), bf16),
            pltpu.VMEM((chunks, length, cols // chunks), bf16),
            dma((5,)),
            dma((n - 1, V_SUB, 4)),
            dma((n - 1, V_SUB, 4)),
            dma((n - 1, O_SUB, 4)),
            dma((n - 1, O_SUB, 4)),
            dma((2, n - 1)),
            dma((2, n - 1)),
            dma((chunks,)),
            dma((chunks,)),
        ],
        compiler_params=pltpu.CompilerParams(
            collective_id=0, has_side_effects=True, vmem_limit_bytes=48 * 2**20),
        cost_estimate=pl.CostEstimate(
            flops=4 * length * cols * n * width, bytes_accessed=2 * 4 * n * cols * width,
            transcendentals=length * LEN * width // HEAD_SIZE),
        name="weights_to_activations",
    )(inputs, queries, keys, w_value, w_out)


def by_activations(inputs, queries, keys, w_value, w_out):
    activ = inputs[0]
    weight_v = w_value[0]
    weight_o = w_out[0]
    length = activ.shape[0]
    col_width = activ.shape[1]
    features_all = lax.all_gather(activ, "tensor", axis=1, tiled=True)
    values = jnp.dot(features_all, weight_v, preferred_element_type=jnp.float32)
    values = values.astype(jnp.bfloat16)
    heads_here = weight_v.shape[1] // HEAD_SIZE
    query_rows = queries[0].reshape(length // LEN, LEN, heads_here, HEAD_SIZE)
    key_rows = keys[0].reshape(length // LEN, LEN, heads_here, HEAD_SIZE)
    value_rows = values.reshape(length // LEN, LEN, heads_here, HEAD_SIZE)
    scores = jnp.einsum(
        "bqhd,bkhd->bhqk", query_rows, key_rows, preferred_element_type=jnp.float32
    ) / jnp.sqrt(jnp.float32(HEAD_SIZE))
    rows = lax.broadcasted_iota(jnp.int32, (LEN, LEN), 0)
    cols = lax.broadcasted_iota(jnp.int32, (LEN, LEN), 1)
    scores = jnp.where((cols <= rows)[None, None], scores, jnp.float32(-1e30))
    top = jnp.max(scores, axis=-1, keepdims=True)
    expo = jnp.exp(scores - top)
    probs = (expo / jnp.sum(expo, axis=-1, keepdims=True)).astype(jnp.bfloat16)
    context = jnp.einsum(
        "bhqk,bkhd->bqhd", probs, value_rows, preferred_element_type=jnp.float32
    ).astype(jnp.bfloat16)
    context = context.reshape(length, heads_here * HEAD_SIZE)
    partial_term = jnp.dot(context, weight_o, preferred_element_type=jnp.float32)
    total = lax.psum_scatter(
        partial_term.astype(jnp.bfloat16), "tensor", scatter_dimension=1, tiled=True)
    result = (total.astype(jnp.float32) + activ.astype(jnp.float32)).astype(jnp.bfloat16)
    size = lax.axis_size("section")
    return lax.ppermute(result, "section", [(i, i ^ 1) for i in range(size)])[None]


def solution(mesh):
    n = mesh.shape["tensor"]

    def on_device(inputs, queries, keys, w_value, w_out):
        length, cols = inputs.shape[1:]
        width = w_value.shape[2]
        weights_smaller = n * width <= mesh.shape["dp"] * length
        divides = (cols % (4 * 128 * O_SUB) == 0 and cols % (4 * 16 * V_SUB) == 0
                   and length % LEN == 0 and n == len(ORDER) + 1 and mesh.shape["dp"] == 4)
        if weights_smaller and divides:
            return by_weights(n, inputs, queries, keys, w_value, w_out)
        return by_activations(inputs, queries, keys, w_value, w_out)

    return jax.shard_map(
        on_device,
        mesh=mesh,
        in_specs=(
            P("section", "dp", "tensor"),
            P("section", "dp", "tensor"),
            P("section", "dp", "tensor"),
            P("section", None, "tensor"),
            P("section", "tensor", None),
        ),
        out_specs=P("section", "dp", "tensor"),
        check_vma=False,
    )
```

```python
import functools

import jax
import jax.numpy as jnp
from jax import lax
from jax.experimental import pallas as pl
from jax.experimental.pallas import tpu as pltpu
from jax.sharding import PartitionSpec as P

HEAD_SIZE = 128
LEN = 256
V_SUB = 3
O_SUB = 3
V_WINDOW = 4
O_WINDOW = 4
EARLY = 1
ORDER = (2, 1, 3)


def flip(index, bit):
    step = 2**bit
    return index + step - 2 * step * lax.rem(index // step, 2)


def flip_by(index, mask):
    for bit in range(mask.bit_length()):
        if mask >> bit & 1:
            index = flip(index, bit)
    return index


def moving_weights(
    n,
    activ_hbm, query_hbm, key_hbm, wv_hbm, wo_hbm, out_hbm,
    activ, query, key, wv, wo, probs, own_part, part_out, part_in, context, result,
    local_sem, wv_send, wv_recv, wo_send, wo_recv, small_send, small_recv, out_send, out_recv,
):
    section = lax.axis_index("section")
    dp = lax.axis_index("dp")
    z = lax.axis_index("tensor")
    length, cols = activ.shape
    quarter = cols // 4
    v_rows = quarter // V_SUB
    o_cols = quarter // O_SUB
    core_peer = flip(dp, 0)
    chip_peer = flip(dp, 1)
    diagonal = flip(core_peer, 1)
    quarters = (dp, core_peer, chip_peer, diagonal)
    other = flip(section, 0)

    barrier = pltpu.get_barrier_semaphore()
    for slot in range(1, n):
        pl.semaphore_signal(barrier, inc=1, device_id=(section, dp, flip_by(z, slot)),
                            device_id_type=pl.DeviceIdType.MESH)
    for target in ((section, core_peer, z), (section, chip_peer, z), (other, dp, z)):
        pl.semaphore_signal(barrier, inc=1, device_id=target, device_id_type=pl.DeviceIdType.MESH)

    def remote(src, dst, send, recv, target):
        return pltpu.make_async_remote_copy(
            src_ref=src, dst_ref=dst, send_sem=send, recv_sem=recv,
            device_id=target, device_id_type=pl.DeviceIdType.MESH)

    own = pl.multiple_of(z * cols, cols)
    locals_ = [
        pltpu.make_async_copy(activ_hbm.at[0], activ, local_sem.at[0]),
        pltpu.make_async_copy(query_hbm.at[0], query, local_sem.at[1]),
        pltpu.make_async_copy(key_hbm.at[0], key, local_sem.at[2]),
        pltpu.make_async_copy(wv_hbm.at[0, pl.ds(own, cols), :], wv.at[0], local_sem.at[3]),
        pltpu.make_async_copy(wo_hbm.at[0, :, pl.ds(own, cols)], wo.at[0], local_sem.at[4]),
    ]
    pl.semaphore_wait(barrier, n + 2)

    pieces = [("v", slot, sub) for sub in range(V_SUB) for slot in ORDER[:2]]
    pieces += [("v", slot, sub) for slot in ORDER[2:] for sub in range(V_SUB)]
    n_value = len(pieces)
    pieces += [("o", slot, sub) for sub in range(O_SUB) for slot in ORDER]

    def v_at(slot, which, sub):
        rows = pl.ds(pl.multiple_of(which * quarter + sub * v_rows, v_rows), v_rows)
        return wv.at[slot, rows, :]

    def o_at(slot, which, sub):
        columns = pl.ds(pl.multiple_of(which * quarter + sub * o_cols, o_cols), o_cols)
        return wo.at[slot, :, columns]

    def copies(piece):
        kind, slot, sub = piece
        peer = flip_by(z, slot)
        if kind == "v":
            start = pl.multiple_of(peer * cols + dp * quarter + sub * v_rows, v_rows)
            source = wv_hbm.at[0, pl.ds(start, v_rows), :]
            at, send, recv = v_at, wv_send, wv_recv
        else:
            start = pl.multiple_of(peer * cols + dp * quarter + sub * o_cols, o_cols)
            source = wo_hbm.at[0, :, pl.ds(start, o_cols)]
            at, send, recv = o_at, wo_send, wo_recv
        mine, far = at(slot, dp, sub), at(slot, chip_peer, sub)
        def sems(hop):
            return send.at[slot - 1, sub, hop], recv.at[slot - 1, sub, hop]
        return (
            remote(source, mine, *sems(0), (section, dp, peer)),
            remote(mine, mine, *sems(1), (section, core_peer, z)),
            remote(mine, mine, *sems(2), (section, chip_peer, z)),
            remote(far, far, *sems(3), (section, core_peer, z)),
        )

    plan = [copies(piece) for piece in pieces]
    n_early = n_value + EARLY * (n - 1)
    for i in range(V_WINDOW):
        plan[i][0].start()
    for copy in locals_:
        copy.start()

    def pass_on(i):
        plan[i][0].wait_recv()
        plan[i][2].start()
        plan[i][1].start()

    def send_after(i, later, end):
        if later < end:
            plan[i][0].wait_send()
            sent.add(i)
            plan[later][0].start()

    def relay(i):
        plan[i][2].wait_recv()
        plan[i][3].start()

    sent = set()

    locals_[1].wait()
    locals_[2].wait()
    causal = lax.broadcasted_iota(jnp.int32, (LEN, LEN), 1) <= lax.broadcasted_iota(jnp.int32, (LEN, LEN), 0)
    scale = 1.0 / HEAD_SIZE**0.5
    heads = query.shape[1] // HEAD_SIZE
    blocks = [(start, head) for start in range(0, length, LEN) for head in range(heads)]
    for at, (start, head) in enumerate(blocks):
        rows, span = slice(start, start + LEN), slice(head * HEAD_SIZE, (head + 1) * HEAD_SIZE)
        scores = lax.dot_general(query[rows, span], key[rows, span], (((1,), (1,)), ((), ())),
                                 preferred_element_type=jnp.float32) * scale
        scores = jnp.where(causal, scores, -1e30)
        expo = jnp.exp(scores - jnp.max(scores, axis=-1, keepdims=True))
        probs[at] = (expo / jnp.sum(expo, axis=-1, keepdims=True)).astype(jnp.bfloat16)
    locals_[0].wait()
    locals_[3].wait()
    own_part[...] = jnp.dot(activ[...], wv[0], preferred_element_type=jnp.float32)

    value_sends = []

    def send_value(slot):
        for i, (kind, at, _) in enumerate(pieces):
            if kind == "v" and at == slot:
                plan[i][1].wait_recv()
                plan[i][3].wait_recv()
        part_out[slot - 1] = jnp.dot(
            activ[...], wv[slot], preferred_element_type=jnp.float32).astype(jnp.bfloat16)
        copy = remote(part_out.at[slot - 1], part_in.at[slot - 1], small_send.at[0, slot - 1],
                      small_recv.at[0, slot - 1], (section, dp, flip_by(z, slot)))
        copy.start()
        value_sends.append(copy)

    last_of = {slot: max(i for i, p in enumerate(pieces) if p[:2] == ("v", slot)) for slot in range(1, n)}
    for i in range(n_value):
        pass_on(i)
        send_after(i, i + V_WINDOW, n_value)
        if i > 0:
            relay(i - 1)
        for slot in range(1, n):
            if last_of[slot] == i - 2:
                send_value(slot)
    for i in range(n_value, n_early):
        plan[i][0].start()
    relay(n_value - 1)
    for slot in ORDER:
        if last_of[slot] > n_value - 3:
            send_value(slot)

    total = own_part[...]
    for copy in value_sends:
        copy.wait_recv()
    for slot in range(1, n):
        total = total + part_in[slot - 1].astype(jnp.float32)
    values = total.astype(jnp.bfloat16)
    for at, (start, head) in enumerate(blocks):
        rows, span = slice(start, start + LEN), slice(head * HEAD_SIZE, (head + 1) * HEAD_SIZE)
        context[0, rows, span] = jnp.dot(
            probs[at], values[rows, span], preferred_element_type=jnp.float32).astype(jnp.bfloat16)

    context_sends = []
    for slot in ORDER:
        copy = remote(context.at[0], context.at[slot], small_send.at[1, slot - 1],
                      small_recv.at[1, slot - 1], (section, dp, flip_by(z, slot)))
        copy.start()
        context_sends.append(copy)
    started = min(n_early + O_WINDOW, len(plan))
    for i in range(n_early, started):
        plan[i][0].start()

    out_sends = []

    def chunk(sub, order):
        first = n_value + sub * (n - 1)
        for i in range(first, first + n - 1):
            if order == 1:
                plan[i][1].wait_recv()
            elif order == 3:
                plan[i][3].wait_recv()
        start = pl.multiple_of(quarters[order] * quarter + sub * o_cols, o_cols)
        columns = pl.ds(start, o_cols)
        total = activ[:, columns].astype(jnp.float32)
        for slot in range(n):
            total = total + jnp.dot(context[slot], wo[slot, :, columns],
                                    preferred_element_type=jnp.float32)
        result[sub * 4 + order] = total.astype(jnp.bfloat16)
        copy = remote(result.at[sub * 4 + order], out_hbm.at[0, :, columns],
                      out_send.at[sub * 4 + order], out_recv.at[sub * 4 + order], (other, dp, z))
        copy.start()
        out_sends.append(copy)

    def bring(sub):
        nonlocal started
        first = n_value + sub * (n - 1)
        for i in range(first, first + n - 1):
            pass_on(i)
            if i >= n_early and started < len(plan):
                send_after(i, started, len(plan))
                started += 1
            if i > first:
                relay(i - 1)

    locals_[4].wait()
    for sub in range(EARLY):
        bring(sub)
        relay(n_value + (sub + 1) * (n - 1) - 1)
    for copy in context_sends:
        copy.wait_recv()
    for sub in range(O_SUB):
        if sub >= EARLY:
            bring(sub)
        chunk(sub, 0)
        chunk(sub, 1)
        if sub >= EARLY:
            relay(n_value + (sub + 1) * (n - 1) - 1)
        chunk(sub, 2)
        chunk(sub, 3)

    for i, piece in enumerate(plan):
        if i not in sent:
            piece[0].wait_send()
        for copy in piece[1:]:
            copy.wait_send()
    for copy in value_sends + context_sends:
        copy.wait_send()
    for copy in out_sends:
        copy.wait()


def by_weights(n, inputs, queries, keys, w_value, w_out):
    length, cols = inputs.shape[1:]
    width = w_value.shape[2]
    bf16, dma = jnp.bfloat16, pltpu.SemaphoreType.DMA
    chunks = 4 * O_SUB
    return pl.pallas_call(
        functools.partial(moving_weights, n),
        out_shape=jax.ShapeDtypeStruct(inputs.shape, bf16),
        in_specs=[pl.BlockSpec(memory_space=pl.ANY)] * 5,
        out_specs=pl.BlockSpec(memory_space=pl.ANY),
        scratch_shapes=[
            pltpu.VMEM((length, cols), bf16),
            pltpu.VMEM((length, width), bf16),
            pltpu.VMEM((length, width), bf16),
            pltpu.VMEM((n, cols, width), bf16),
            pltpu.VMEM((n, width, cols), bf16),
            pltpu.VMEM((length // LEN * width // HEAD_SIZE, LEN, LEN), bf16),
            pltpu.VMEM((length, width), jnp.float32),
            pltpu.VMEM((n - 1, length, width), bf16),
            pltpu.VMEM((n - 1, length, width), bf16),
            pltpu.VMEM((n, length, width), bf16),
            pltpu.VMEM((chunks, length, cols // chunks), bf16),
            dma((5,)),
            dma((n - 1, V_SUB, 4)),
            dma((n - 1, V_SUB, 4)),
            dma((n - 1, O_SUB, 4)),
            dma((n - 1, O_SUB, 4)),
            dma((2, n - 1)),
            dma((2, n - 1)),
            dma((chunks,)),
            dma((chunks,)),
        ],
        compiler_params=pltpu.CompilerParams(
            collective_id=0, has_side_effects=True, vmem_limit_bytes=60 * 2**20),
        cost_estimate=pl.CostEstimate(
            flops=4 * length * cols * n * width, bytes_accessed=2 * 4 * n * cols * width,
            transcendentals=length * LEN * width // HEAD_SIZE),
        name="weights_to_activations",
    )(inputs, queries, keys, w_value, w_out)


def by_activations(inputs, queries, keys, w_value, w_out):
    activ = inputs[0]
    weight_v = w_value[0]
    weight_o = w_out[0]
    length = activ.shape[0]
    col_width = activ.shape[1]
    features_all = lax.all_gather(activ, "tensor", axis=1, tiled=True)
    values = jnp.dot(features_all, weight_v, preferred_element_type=jnp.float32)
    values = values.astype(jnp.bfloat16)
    heads_here = weight_v.shape[1] // HEAD_SIZE
    query_rows = queries[0].reshape(length // LEN, LEN, heads_here, HEAD_SIZE)
    key_rows = keys[0].reshape(length // LEN, LEN, heads_here, HEAD_SIZE)
    value_rows = values.reshape(length // LEN, LEN, heads_here, HEAD_SIZE)
    scores = jnp.einsum(
        "bqhd,bkhd->bhqk", query_rows, key_rows, preferred_element_type=jnp.float32
    ) / jnp.sqrt(jnp.float32(HEAD_SIZE))
    rows = lax.broadcasted_iota(jnp.int32, (LEN, LEN), 0)
    cols = lax.broadcasted_iota(jnp.int32, (LEN, LEN), 1)
    scores = jnp.where((cols <= rows)[None, None], scores, jnp.float32(-1e30))
    top = jnp.max(scores, axis=-1, keepdims=True)
    expo = jnp.exp(scores - top)
    probs = (expo / jnp.sum(expo, axis=-1, keepdims=True)).astype(jnp.bfloat16)
    context = jnp.einsum(
        "bhqk,bkhd->bqhd", probs, value_rows, preferred_element_type=jnp.float32
    ).astype(jnp.bfloat16)
    context = context.reshape(length, heads_here * HEAD_SIZE)
    partial_term = jnp.dot(context, weight_o, preferred_element_type=jnp.float32)
    total = lax.psum_scatter(
        partial_term.astype(jnp.bfloat16), "tensor", scatter_dimension=1, tiled=True)
    result = (total.astype(jnp.float32) + activ.astype(jnp.float32)).astype(jnp.bfloat16)
    size = lax.axis_size("section")
    return lax.ppermute(result, "section", [(i, i ^ 1) for i in range(size)])[None]


def solution(mesh):
    n = mesh.shape["tensor"]

    def on_device(inputs, queries, keys, w_value, w_out):
        length, cols = inputs.shape[1:]
        width = w_value.shape[2]
        weights_smaller = n * width <= mesh.shape["dp"] * length
        divides = (cols % (4 * 128 * O_SUB) == 0 and cols % (4 * 16 * V_SUB) == 0
                   and length % LEN == 0 and n == len(ORDER) + 1 and mesh.shape["dp"] == 4)
        if weights_smaller and divides:
            return by_weights(n, inputs, queries, keys, w_value, w_out)
        return by_activations(inputs, queries, keys, w_value, w_out)

    return jax.shard_map(
        on_device,
        mesh=mesh,
        in_specs=(
            P("section", "dp", "tensor"),
            P("section", "dp", "tensor"),
            P("section", "dp", "tensor"),
            P("section", None, "tensor"),
            P("section", "tensor", None),
        ),
        out_specs=P("section", "dp", "tensor"),
        check_vma=False,
    )
```

```python
import functools

import jax
import jax.numpy as jnp
from jax import lax
from jax.experimental import pallas as pl
from jax.experimental.pallas import tpu as pltpu
from jax.sharding import PartitionSpec as P

HEAD_SIZE = 128
LEN = 256
V_SUB = 3
O_SHARES = (1, 1, 2, 1, 1)
O_SUB, O_UNITS = len(O_SHARES), sum(O_SHARES)
V_WINDOW = 4
O_WINDOW = 6
GROUP = 4


def flip(index, bit):
    step = 2**bit
    return index + step - 2 * step * lax.rem(index // step, 2)


def flip_by(index, mask):
    for bit in range(mask.bit_length()):
        if mask >> bit & 1:
            index = flip(index, bit)
    return index


def moving_weights(
    n,
    activ_hbm, query_hbm, key_hbm, wv_hbm, wo_hbm, out_hbm,
    activ, query, key, wv, wo, probs, own_part, part_out, part_in, context, result,
    local_sem, wv_send, wv_recv, wo_send, wo_recv, small_send, small_recv, out_send, out_recv,
):
    section = lax.axis_index("section")
    dp = lax.axis_index("dp")
    z = lax.axis_index("tensor")
    length, cols = activ.shape
    quarter = cols // 4
    v_rows = quarter // V_SUB
    unit = quarter // O_UNITS
    o_start = [sum(O_SHARES[:sub]) * unit for sub in range(O_SUB)]
    o_cols = [share * unit for share in O_SHARES]
    core_peer = flip(dp, 0)
    chip_peer = flip(dp, 1)
    diagonal = flip(core_peer, 1)
    quarters = (dp, core_peer, chip_peer, diagonal)
    other = flip(section, 0)

    barrier = pltpu.get_barrier_semaphore()
    for slot in range(1, n):
        pl.semaphore_signal(barrier, inc=1, device_id=(section, dp, flip_by(z, slot)),
                            device_id_type=pl.DeviceIdType.MESH)
    for target in ((section, core_peer, z), (section, chip_peer, z), (other, dp, z)):
        pl.semaphore_signal(barrier, inc=1, device_id=target, device_id_type=pl.DeviceIdType.MESH)

    def remote(src, dst, send, recv, target):
        return pltpu.make_async_remote_copy(
            src_ref=src, dst_ref=dst, send_sem=send, recv_sem=recv,
            device_id=target, device_id_type=pl.DeviceIdType.MESH)

    own = pl.multiple_of(z * cols, cols)
    locals_ = [
        pltpu.make_async_copy(activ_hbm.at[0], activ, local_sem.at[0]),
        pltpu.make_async_copy(query_hbm.at[0], query, local_sem.at[1]),
        pltpu.make_async_copy(key_hbm.at[0], key, local_sem.at[2]),
        pltpu.make_async_copy(wv_hbm.at[0, pl.ds(own, cols), :], wv.at[0], local_sem.at[3]),
        pltpu.make_async_copy(wo_hbm.at[0, :, pl.ds(own, cols)], wo.at[0], local_sem.at[4]),
    ]
    pl.semaphore_wait(barrier, n + 2)

    pieces = [("v", 3, sub) for sub in range(V_SUB)]
    pieces += [("v", slot, sub) for sub in range(V_SUB) for slot in (2, 1)]
    n_value = len(pieces)
    pieces += [("o", slot, sub) for sub in range(O_SUB) for slot in (3, 2, 1)]

    def v_at(slot, which, sub):
        rows = pl.ds(pl.multiple_of(which * quarter + sub * v_rows, v_rows), v_rows)
        return wv.at[slot, rows, :]

    def o_at(slot, which, sub):
        columns = pl.ds(pl.multiple_of(which * quarter + o_start[sub], unit), o_cols[sub])
        return wo.at[slot, :, columns]

    def copies(piece):
        kind, slot, sub = piece
        peer = flip_by(z, slot)
        if kind == "v":
            start = pl.multiple_of(peer * cols + dp * quarter + sub * v_rows, v_rows)
            source = wv_hbm.at[0, pl.ds(start, v_rows), :]
            at, send, recv = v_at, wv_send, wv_recv
        else:
            start = pl.multiple_of(peer * cols + dp * quarter + o_start[sub], unit)
            source = wo_hbm.at[0, :, pl.ds(start, o_cols[sub])]
            at, send, recv = o_at, wo_send, wo_recv
        mine, far = at(slot, dp, sub), at(slot, chip_peer, sub)
        def sems(hop):
            return send.at[slot - 1, sub, hop], recv.at[slot - 1, sub, hop]
        return (
            remote(source, mine, *sems(0), (section, dp, peer)),
            remote(mine, mine, *sems(1), (section, core_peer, z)),
            remote(mine, mine, *sems(2), (section, chip_peer, z)),
            remote(far, far, *sems(3), (section, core_peer, z)),
        )

    plan = [copies(piece) for piece in pieces]
    for i in range(V_WINDOW):
        plan[i][0].start()
    for copy in locals_:
        copy.start()

    def pass_on(i):
        plan[i][0].wait_recv()
        plan[i][2].start()
        plan[i][1].start()

    def relay(i):
        plan[i][2].wait_recv()
        plan[i][3].start()

    locals_[1].wait()
    locals_[2].wait()
    causal = lax.broadcasted_iota(jnp.int32, (LEN, LEN), 1) <= lax.broadcasted_iota(jnp.int32, (LEN, LEN), 0)
    scale = 1.0 / HEAD_SIZE**0.5
    heads = query.shape[1] // HEAD_SIZE
    blocks = [(start, head) for start in range(0, length, LEN) for head in range(heads)]
    for at, (start, head) in enumerate(blocks):
        rows, span = slice(start, start + LEN), slice(head * HEAD_SIZE, (head + 1) * HEAD_SIZE)
        scores = lax.dot_general(query[rows, span], key[rows, span], (((1,), (1,)), ((), ())),
                                 preferred_element_type=jnp.float32) * scale
        scores = jnp.where(causal, scores, -1e30)
        expo = jnp.exp(scores - jnp.max(scores, axis=-1, keepdims=True))
        probs[at] = (expo / jnp.sum(expo, axis=-1, keepdims=True)).astype(jnp.bfloat16)
    locals_[0].wait()
    locals_[3].wait()
    own_part[...] = jnp.dot(activ[...], wv[0], preferred_element_type=jnp.float32)

    near, across = flip_by(z, 1), flip_by(z, 2)
    value_copies = [
        remote(part_out.at[m], part_in.at[m], small_send.at[0, m], small_recv.at[0, m], (section, dp, to))
        for m, to in enumerate((near, across, near))]

    def send_value(slot):
        for i, (kind, at, _) in enumerate(pieces):
            if kind == "v" and at == slot:
                plan[i][1].wait_recv()
                plan[i][3].wait_recv()
        term = jnp.dot(activ[...], wv[slot], preferred_element_type=jnp.float32)
        if slot == 2:
            value_copies[0].wait_recv()
            term = term + part_in[0].astype(jnp.float32)
        part_out[3 - slot] = term.astype(jnp.bfloat16)
        value_copies[3 - slot].start()

    for i in range(n_value):
        pass_on(i)
        if i + V_WINDOW < n_value:
            plan[i][0].wait_send()
            plan[i + V_WINDOW][0].start()
        if i > 0:
            relay(i - 1)
        if i == V_SUB + 1:
            send_value(3)

    def piece_range(sub):
        first = n_value + sub * (n - 1)
        return range(first, first + n - 1)

    for i in piece_range(0):
        plan[i][0].start()
    relay(n_value - 1)
    send_value(2)
    send_value(1)
    for i in piece_range(1):
        plan[i][0].start()
    for i in piece_range(0):
        pass_on(i)

    value_copies[1].wait_recv()
    value_copies[2].wait_recv()
    total = own_part[...] + part_in[1].astype(jnp.float32) + part_in[2].astype(jnp.float32)
    values = total.astype(jnp.bfloat16)
    for at, (start, head) in enumerate(blocks):
        rows, span = slice(start, start + LEN), slice(head * HEAD_SIZE, (head + 1) * HEAD_SIZE)
        context[0, rows, span] = jnp.dot(
            probs[at], values[rows, span], preferred_element_type=jnp.float32).astype(jnp.bfloat16)

    context_copies = [
        remote(context.at[src], context.at[dst], small_send.at[1, m], small_recv.at[1, m], (section, dp, to))
        for m, (src, dst, to) in enumerate(((0, 2, across), (0, 1, near), (2, 3, near)))]
    context_copies[0].start()
    context_copies[1].start()
    started = min(n_value + 2 * (n - 1) + O_WINDOW, len(plan))
    for i in range(n_value + 2 * (n - 1), started):
        plan[i][0].start()
    for i in piece_range(0):
        relay(i)
    for i in piece_range(1):
        pass_on(i)
    context_copies[0].wait_recv()
    context_copies[2].start()
    for i in piece_range(1):
        relay(i)
    locals_[4].wait()
    context_copies[1].wait_recv()
    context_copies[2].wait_recv()

    out_sends = []

    def chunk(sub, order):
        for i in piece_range(sub):
            if order == 1:
                plan[i][1].wait_recv()
            elif order == 3:
                plan[i][3].wait_recv()
        columns = pl.ds(pl.multiple_of(quarters[order] * quarter + o_start[sub], unit), o_cols[sub])
        total = activ[:, columns].astype(jnp.float32)
        for slot in range(n):
            total = total + jnp.dot(context[slot], wo[slot, :, columns],
                                    preferred_element_type=jnp.float32)
        result[:, columns] = total.astype(jnp.bfloat16)
        copy = remote(result.at[:, columns], out_hbm.at[0, :, columns],
                      out_send.at[sub, order], out_recv.at[sub, order], (other, dp, z))
        copy.start()
        out_sends.append(copy)

    for sub in range(O_SUB):
        if sub >= 2:
            for i in piece_range(sub):
                pass_on(i)
                if started < len(plan):
                    plan[started][0].start()
                    started += 1
                if i > piece_range(sub)[0]:
                    relay(i - 1)
        chunk(sub, 0)
        chunk(sub, 1)
        if sub >= 2:
            relay(piece_range(sub)[-1])
        chunk(sub, 2)
        chunk(sub, 3)

    for i, piece in enumerate(plan):
        if not i + V_WINDOW < n_value:
            piece[0].wait_send()
        for copy in piece[1:]:
            copy.wait_send()
    for copy in value_copies + context_copies:
        copy.wait_send()
    for copy in out_sends:
        copy.wait()


def by_weights(n, inputs, queries, keys, w_value, w_out):
    length, cols = inputs.shape[1:]
    width = w_value.shape[2]
    bf16, dma = jnp.bfloat16, pltpu.SemaphoreType.DMA
    return pl.pallas_call(
        functools.partial(moving_weights, n),
        out_shape=jax.ShapeDtypeStruct(inputs.shape, bf16),
        in_specs=[pl.BlockSpec(memory_space=pl.ANY)] * 5,
        out_specs=pl.BlockSpec(memory_space=pl.ANY),
        scratch_shapes=[
            pltpu.VMEM((length, cols), bf16),
            pltpu.VMEM((length, width), bf16),
            pltpu.VMEM((length, width), bf16),
            pltpu.VMEM((n, cols, width), bf16),
            pltpu.VMEM((n, width, cols), bf16),
            pltpu.VMEM((length // LEN * width // HEAD_SIZE, LEN, LEN), bf16),
            pltpu.VMEM((length, width), jnp.float32),
            pltpu.VMEM((n - 1, length, width), bf16),
            pltpu.VMEM((n - 1, length, width), bf16),
            pltpu.VMEM((n, length, width), bf16),
            pltpu.VMEM((length, cols), bf16),
            dma((5,)),
            dma((n - 1, V_SUB, 4)),
            dma((n - 1, V_SUB, 4)),
            dma((n - 1, O_SUB, 4)),
            dma((n - 1, O_SUB, 4)),
            dma((2, n - 1)),
            dma((2, n - 1)),
            dma((O_SUB, 4)),
            dma((O_SUB, 4)),
        ],
        compiler_params=pltpu.CompilerParams(
            collective_id=0, has_side_effects=True, vmem_limit_bytes=60 * 2**20),
        cost_estimate=pl.CostEstimate(
            flops=4 * length * cols * n * width, bytes_accessed=2 * 4 * n * cols * width,
            transcendentals=length * LEN * width // HEAD_SIZE),
        name="weights_to_activations",
    )(inputs, queries, keys, w_value, w_out)


def by_activations(inputs, queries, keys, w_value, w_out):
    activ = inputs[0]
    weight_v = w_value[0]
    weight_o = w_out[0]
    length = activ.shape[0]
    col_width = activ.shape[1]
    features_all = lax.all_gather(activ, "tensor", axis=1, tiled=True)
    values = jnp.dot(features_all, weight_v, preferred_element_type=jnp.float32)
    values = values.astype(jnp.bfloat16)
    heads_here = weight_v.shape[1] // HEAD_SIZE
    query_rows = queries[0].reshape(length // LEN, LEN, heads_here, HEAD_SIZE)
    key_rows = keys[0].reshape(length // LEN, LEN, heads_here, HEAD_SIZE)
    value_rows = values.reshape(length // LEN, LEN, heads_here, HEAD_SIZE)
    scores = jnp.einsum(
        "bqhd,bkhd->bhqk", query_rows, key_rows, preferred_element_type=jnp.float32
    ) / jnp.sqrt(jnp.float32(HEAD_SIZE))
    rows = lax.broadcasted_iota(jnp.int32, (LEN, LEN), 0)
    cols = lax.broadcasted_iota(jnp.int32, (LEN, LEN), 1)
    scores = jnp.where((cols <= rows)[None, None], scores, jnp.float32(-1e30))
    top = jnp.max(scores, axis=-1, keepdims=True)
    expo = jnp.exp(scores - top)
    probs = (expo / jnp.sum(expo, axis=-1, keepdims=True)).astype(jnp.bfloat16)
    context = jnp.einsum(
        "bhqk,bkhd->bqhd", probs, value_rows, preferred_element_type=jnp.float32
    ).astype(jnp.bfloat16)
    context = context.reshape(length, heads_here * HEAD_SIZE)
    partial_term = jnp.dot(context, weight_o, preferred_element_type=jnp.float32)
    total = lax.psum_scatter(
        partial_term.astype(jnp.bfloat16), "tensor", scatter_dimension=1, tiled=True)
    result = (total.astype(jnp.float32) + activ.astype(jnp.float32)).astype(jnp.bfloat16)
    size = lax.axis_size("section")
    return lax.ppermute(result, "section", [(i, i ^ 1) for i in range(size)])[None]


def solution(mesh):
    n = mesh.shape["tensor"]

    def on_device(inputs, queries, keys, w_value, w_out):
        length, cols = inputs.shape[1:]
        width = w_value.shape[2]
        weights_smaller = n * width <= mesh.shape["dp"] * length
        divides = (cols % (4 * 128 * O_UNITS) == 0 and cols % (4 * 16 * V_SUB) == 0
                   and length % LEN == 0 and n == GROUP and mesh.shape["dp"] == 4)
        if weights_smaller and divides:
            return by_weights(n, inputs, queries, keys, w_value, w_out)
        return by_activations(inputs, queries, keys, w_value, w_out)

    return jax.shard_map(
        on_device,
        mesh=mesh,
        in_specs=(
            P("section", "dp", "tensor"),
            P("section", "dp", "tensor"),
            P("section", "dp", "tensor"),
            P("section", None, "tensor"),
            P("section", "tensor", None),
        ),
        out_specs=P("section", "dp", "tensor"),
        check_vma=False,
    )
```

```python
import functools

import jax
import jax.numpy as jnp
from jax import lax
from jax.experimental import pallas as pl
from jax.experimental.pallas import tpu as pltpu
from jax.sharding import PartitionSpec as P

HEAD_SIZE = 128
LEN = 256
V_SUB = 3
O_SHARES = (1, 1, 2, 1, 1)
O_SUB, O_UNITS = len(O_SHARES), sum(O_SHARES)
V_WINDOW = 9
O_WINDOW = 9
GROUP = 4


def flip(index, bit):
    step = 2**bit
    return index + step - 2 * step * lax.rem(index // step, 2)


def flip_by(index, mask):
    for bit in range(mask.bit_length()):
        if mask >> bit & 1:
            index = flip(index, bit)
    return index


def moving_weights(
    n,
    activ_hbm, query_hbm, key_hbm, wv_hbm, wo_hbm, out_hbm,
    activ, query, key, wv, wo, probs, own_part, part_out, part_in, context, result,
    local_sem, wv_send, wv_recv, wo_send, wo_recv, small_send, small_recv, out_send, out_recv,
):
    section = lax.axis_index("section")
    dp = lax.axis_index("dp")
    z = lax.axis_index("tensor")
    length, cols = activ.shape
    quarter = cols // 4
    v_rows = quarter // V_SUB
    unit = quarter // O_UNITS
    o_start = [sum(O_SHARES[:sub]) * unit for sub in range(O_SUB)]
    o_cols = [share * unit for share in O_SHARES]
    core_peer = flip(dp, 0)
    chip_peer = flip(dp, 1)
    diagonal = flip(core_peer, 1)
    quarters = (dp, core_peer, chip_peer, diagonal)
    other = flip(section, 0)

    barrier = pltpu.get_barrier_semaphore()
    for slot in range(1, n):
        pl.semaphore_signal(barrier, inc=1, device_id=(section, dp, flip_by(z, slot)),
                            device_id_type=pl.DeviceIdType.MESH)
    for target in ((section, core_peer, z), (section, chip_peer, z), (other, dp, z)):
        pl.semaphore_signal(barrier, inc=1, device_id=target, device_id_type=pl.DeviceIdType.MESH)

    def remote(src, dst, send, recv, target):
        return pltpu.make_async_remote_copy(
            src_ref=src, dst_ref=dst, send_sem=send, recv_sem=recv,
            device_id=target, device_id_type=pl.DeviceIdType.MESH)

    own = pl.multiple_of(z * cols, cols)
    locals_ = [
        pltpu.make_async_copy(activ_hbm.at[0], activ, local_sem.at[0]),
        pltpu.make_async_copy(query_hbm.at[0], query, local_sem.at[1]),
        pltpu.make_async_copy(key_hbm.at[0], key, local_sem.at[2]),
        pltpu.make_async_copy(wv_hbm.at[0, pl.ds(own, cols), :], wv.at[0], local_sem.at[3]),
        pltpu.make_async_copy(wo_hbm.at[0, :, pl.ds(own, cols)], wo.at[0], local_sem.at[4]),
    ]
    pl.semaphore_wait(barrier, n + 2)

    pieces = [("v", 3, sub) for sub in range(V_SUB)]
    pieces += [("v", slot, sub) for sub in range(V_SUB) for slot in (2, 1)]
    n_value = len(pieces)
    pieces += [("o", slot, sub) for sub in range(O_SUB) for slot in (3, 2, 1)]

    def v_at(slot, which, sub):
        rows = pl.ds(pl.multiple_of(which * quarter + sub * v_rows, v_rows), v_rows)
        return wv.at[slot, rows, :]

    def o_at(slot, which, sub):
        columns = pl.ds(pl.multiple_of(which * quarter + o_start[sub], unit), o_cols[sub])
        return wo.at[slot, :, columns]

    def copies(piece):
        kind, slot, sub = piece
        peer = flip_by(z, slot)
        if kind == "v":
            start = pl.multiple_of(peer * cols + dp * quarter + sub * v_rows, v_rows)
            source = wv_hbm.at[0, pl.ds(start, v_rows), :]
            at, send, recv = v_at, wv_send, wv_recv
        else:
            start = pl.multiple_of(peer * cols + dp * quarter + o_start[sub], unit)
            source = wo_hbm.at[0, :, pl.ds(start, o_cols[sub])]
            at, send, recv = o_at, wo_send, wo_recv
        mine, far = at(slot, dp, sub), at(slot, chip_peer, sub)
        def sems(hop):
            return send.at[slot - 1, sub, hop], recv.at[slot - 1, sub, hop]
        return (
            remote(source, mine, *sems(0), (section, dp, peer)),
            remote(mine, mine, *sems(1), (section, core_peer, z)),
            remote(mine, mine, *sems(2), (section, chip_peer, z)),
            remote(far, far, *sems(3), (section, core_peer, z)),
        )

    plan = [copies(piece) for piece in pieces]
    for i in range(V_WINDOW):
        plan[i][0].start()
    for copy in locals_:
        copy.start()

    def pass_on(i):
        plan[i][0].wait_recv()
        plan[i][2].start()
        plan[i][1].start()

    def relay(i):
        plan[i][2].wait_recv()
        plan[i][3].start()

    locals_[1].wait()
    locals_[2].wait()
    causal = lax.broadcasted_iota(jnp.int32, (LEN, LEN), 1) <= lax.broadcasted_iota(jnp.int32, (LEN, LEN), 0)
    scale = 1.0 / HEAD_SIZE**0.5
    heads = query.shape[1] // HEAD_SIZE
    blocks = [(start, head) for start in range(0, length, LEN) for head in range(heads)]
    for at, (start, head) in enumerate(blocks):
        rows, span = slice(start, start + LEN), slice(head * HEAD_SIZE, (head + 1) * HEAD_SIZE)
        scores = lax.dot_general(query[rows, span], key[rows, span], (((1,), (1,)), ((), ())),
                                 preferred_element_type=jnp.float32) * scale
        scores = jnp.where(causal, scores, -1e30)
        expo = jnp.exp(scores - jnp.max(scores, axis=-1, keepdims=True))
        probs[at] = (expo / jnp.sum(expo, axis=-1, keepdims=True)).astype(jnp.bfloat16)
    locals_[0].wait()
    locals_[3].wait()
    own_part[...] = jnp.dot(activ[...], wv[0], preferred_element_type=jnp.float32)

    near, across = flip_by(z, 1), flip_by(z, 2)
    value_copies = [
        remote(part_out.at[m], part_in.at[m], small_send.at[0, m], small_recv.at[0, m], (section, dp, to))
        for m, to in enumerate((near, across, near))]

    def send_value(slot):
        for i, (kind, at, _) in enumerate(pieces):
            if kind == "v" and at == slot:
                plan[i][1].wait_recv()
                plan[i][3].wait_recv()
        term = jnp.dot(activ[...], wv[slot], preferred_element_type=jnp.float32)
        if slot == 2:
            value_copies[0].wait_recv()
            term = term + part_in[0].astype(jnp.float32)
        part_out[3 - slot] = term.astype(jnp.bfloat16)
        value_copies[3 - slot].start()

    for i in range(n_value):
        pass_on(i)
        if i + V_WINDOW < n_value:
            plan[i][0].wait_send()
            plan[i + V_WINDOW][0].start()
        if i > 1:
            relay(i - 2)
        if i == V_SUB + 2:
            send_value(3)

    def piece_range(sub):
        first = n_value + sub * (n - 1)
        return range(first, first + n - 1)

    for i in piece_range(0):
        plan[i][0].start()
    relay(n_value - 2)
    relay(n_value - 1)
    send_value(2)
    send_value(1)
    for i in piece_range(1):
        plan[i][0].start()
    for i in piece_range(0):
        pass_on(i)

    value_copies[1].wait_recv()
    value_copies[2].wait_recv()
    total = own_part[...] + part_in[1].astype(jnp.float32) + part_in[2].astype(jnp.float32)
    values = total.astype(jnp.bfloat16)
    for at, (start, head) in enumerate(blocks):
        rows, span = slice(start, start + LEN), slice(head * HEAD_SIZE, (head + 1) * HEAD_SIZE)
        context[0, rows, span] = jnp.dot(
            probs[at], values[rows, span], preferred_element_type=jnp.float32).astype(jnp.bfloat16)

    context_copies = [
        remote(context.at[src], context.at[dst], small_send.at[1, m], small_recv.at[1, m], (section, dp, to))
        for m, (src, dst, to) in enumerate(((0, 2, across), (0, 1, near), (2, 3, near)))]
    context_copies[0].start()
    context_copies[1].start()
    started = min(n_value + 2 * (n - 1) + O_WINDOW, len(plan))
    for i in range(n_value + 2 * (n - 1), started):
        plan[i][0].start()
    for i in piece_range(0):
        relay(i)
    for i in piece_range(1):
        pass_on(i)
    context_copies[0].wait_recv()
    context_copies[2].start()
    for i in piece_range(1):
        relay(i)
    locals_[4].wait()
    context_copies[1].wait_recv()
    context_copies[2].wait_recv()

    out_sends = []

    def chunk(sub, order):
        for i in piece_range(sub):
            if order == 1:
                plan[i][1].wait_recv()
            elif order == 3:
                plan[i][3].wait_recv()
        columns = pl.ds(pl.multiple_of(quarters[order] * quarter + o_start[sub], unit), o_cols[sub])
        total = activ[:, columns].astype(jnp.float32)
        for slot in range(n):
            total = total + jnp.dot(context[slot], wo[slot, :, columns],
                                    preferred_element_type=jnp.float32)
        result[:, columns] = total.astype(jnp.bfloat16)
        copy = remote(result.at[:, columns], out_hbm.at[0, :, columns],
                      out_send.at[sub, order], out_recv.at[sub, order], (other, dp, z))
        copy.start()
        out_sends.append(copy)

    for sub in range(O_SUB):
        if sub >= 2:
            for i in piece_range(sub):
                pass_on(i)
                if started < len(plan):
                    plan[started][0].start()
                    started += 1
                if i > piece_range(sub)[0]:
                    relay(i - 1)
        chunk(sub, 0)
        chunk(sub, 1)
        if sub >= 2:
            relay(piece_range(sub)[-1])
        chunk(sub, 2)
        chunk(sub, 3)

    for i, piece in enumerate(plan):
        if not i + V_WINDOW < n_value:
            piece[0].wait_send()
        for copy in piece[1:]:
            copy.wait_send()
    for copy in value_copies + context_copies:
        copy.wait_send()
    for copy in out_sends:
        copy.wait()


def by_weights(n, inputs, queries, keys, w_value, w_out):
    length, cols = inputs.shape[1:]
    width = w_value.shape[2]
    bf16, dma = jnp.bfloat16, pltpu.SemaphoreType.DMA
    return pl.pallas_call(
        functools.partial(moving_weights, n),
        out_shape=jax.ShapeDtypeStruct(inputs.shape, bf16),
        in_specs=[pl.BlockSpec(memory_space=pl.ANY)] * 5,
        out_specs=pl.BlockSpec(memory_space=pl.ANY),
        scratch_shapes=[
            pltpu.VMEM((length, cols), bf16),
            pltpu.VMEM((length, width), bf16),
            pltpu.VMEM((length, width), bf16),
            pltpu.VMEM((n, cols, width), bf16),
            pltpu.VMEM((n, width, cols), bf16),
            pltpu.VMEM((length // LEN * width // HEAD_SIZE, LEN, LEN), bf16),
            pltpu.VMEM((length, width), jnp.float32),
            pltpu.VMEM((n - 1, length, width), bf16),
            pltpu.VMEM((n - 1, length, width), bf16),
            pltpu.VMEM((n, length, width), bf16),
            pltpu.VMEM((length, cols), bf16),
            dma((5,)),
            dma((n - 1, V_SUB, 4)),
            dma((n - 1, V_SUB, 4)),
            dma((n - 1, O_SUB, 4)),
            dma((n - 1, O_SUB, 4)),
            dma((2, n - 1)),
            dma((2, n - 1)),
            dma((O_SUB, 4)),
            dma((O_SUB, 4)),
        ],
        compiler_params=pltpu.CompilerParams(
            collective_id=0, has_side_effects=True, vmem_limit_bytes=60 * 2**20),
        cost_estimate=pl.CostEstimate(
            flops=4 * length * cols * n * width, bytes_accessed=2 * 4 * n * cols * width,
            transcendentals=length * LEN * width // HEAD_SIZE),
        name="weights_to_activations",
    )(inputs, queries, keys, w_value, w_out)


def by_activations(inputs, queries, keys, w_value, w_out):
    activ = inputs[0]
    weight_v = w_value[0]
    weight_o = w_out[0]
    length = activ.shape[0]
    col_width = activ.shape[1]
    features_all = lax.all_gather(activ, "tensor", axis=1, tiled=True)
    values = jnp.dot(features_all, weight_v, preferred_element_type=jnp.float32)
    values = values.astype(jnp.bfloat16)
    heads_here = weight_v.shape[1] // HEAD_SIZE
    query_rows = queries[0].reshape(length // LEN, LEN, heads_here, HEAD_SIZE)
    key_rows = keys[0].reshape(length // LEN, LEN, heads_here, HEAD_SIZE)
    value_rows = values.reshape(length // LEN, LEN, heads_here, HEAD_SIZE)
    scores = jnp.einsum(
        "bqhd,bkhd->bhqk", query_rows, key_rows, preferred_element_type=jnp.float32
    ) / jnp.sqrt(jnp.float32(HEAD_SIZE))
    rows = lax.broadcasted_iota(jnp.int32, (LEN, LEN), 0)
    cols = lax.broadcasted_iota(jnp.int32, (LEN, LEN), 1)
    scores = jnp.where((cols <= rows)[None, None], scores, jnp.float32(-1e30))
    top = jnp.max(scores, axis=-1, keepdims=True)
    expo = jnp.exp(scores - top)
    probs = (expo / jnp.sum(expo, axis=-1, keepdims=True)).astype(jnp.bfloat16)
    context = jnp.einsum(
        "bhqk,bkhd->bqhd", probs, value_rows, preferred_element_type=jnp.float32
    ).astype(jnp.bfloat16)
    context = context.reshape(length, heads_here * HEAD_SIZE)
    partial_term = jnp.dot(context, weight_o, preferred_element_type=jnp.float32)
    total = lax.psum_scatter(
        partial_term.astype(jnp.bfloat16), "tensor", scatter_dimension=1, tiled=True)
    result = (total.astype(jnp.float32) + activ.astype(jnp.float32)).astype(jnp.bfloat16)
    size = lax.axis_size("section")
    return lax.ppermute(result, "section", [(i, i ^ 1) for i in range(size)])[None]


def solution(mesh):
    n = mesh.shape["tensor"]

    def on_device(inputs, queries, keys, w_value, w_out):
        length, cols = inputs.shape[1:]
        width = w_value.shape[2]
        weights_smaller = n * width <= mesh.shape["dp"] * length
        divides = (cols % (4 * 128 * O_UNITS) == 0 and cols % (4 * 16 * V_SUB) == 0
                   and length % LEN == 0 and n == GROUP and mesh.shape["dp"] == 4)
        if weights_smaller and divides:
            return by_weights(n, inputs, queries, keys, w_value, w_out)
        return by_activations(inputs, queries, keys, w_value, w_out)

    return jax.shard_map(
        on_device,
        mesh=mesh,
        in_specs=(
            P("section", "dp", "tensor"),
            P("section", "dp", "tensor"),
            P("section", "dp", "tensor"),
            P("section", None, "tensor"),
            P("section", "tensor", None),
        ),
        out_specs=P("section", "dp", "tensor"),
        check_vma=False,
    )
```

```python
import functools

import jax
import jax.numpy as jnp
from jax import lax
from jax.experimental import pallas as pl
from jax.experimental.pallas import tpu as pltpu
from jax.sharding import PartitionSpec as P

HEAD_SIZE = 128
LEN = 256
V_SUB = 3
O_SHARES = (2, 2, 1, 1)
O_SUB, O_UNITS = len(O_SHARES), sum(O_SHARES)
WINDOW = 4
GROUP = 4


def flip(index, bit):
    step = 2**bit
    return index + step - 2 * step * lax.rem(index // step, 2)


def flip_by(index, mask):
    for bit in range(mask.bit_length()):
        if mask >> bit & 1:
            index = flip(index, bit)
    return index


def moving_weights(
    n,
    activ_hbm, query_hbm, key_hbm, wv_hbm, wo_hbm, out_hbm,
    activ, residual, query, key, wv, wo, probs, own_part, part_out, part_in, own_context, context, result,
    local_sem, residual_sem, wv_send, wv_recv, wo_send, wo_recv, value_send, value_recv, context_send, context_recv, out_sem,
):
    section = lax.axis_index("section")
    dp = lax.axis_index("dp")
    z = lax.axis_index("tensor")
    length, cols = activ.shape
    quarter = cols // 4
    v_rows = quarter // V_SUB
    unit = quarter // O_UNITS
    o_start = [sum(O_SHARES[:sub]) * unit for sub in range(O_SUB)]
    o_cols = [share * unit for share in O_SHARES]
    core_peer = flip(dp, 0)
    chip_peer = flip(dp, 1)
    diagonal = flip(core_peer, 1)
    quarters = (dp, core_peer, chip_peer, diagonal)
    other = flip(section, 0)

    barrier = pltpu.get_barrier_semaphore()
    for slot in range(1, n):
        pl.semaphore_signal(barrier, inc=1, device_id=(section, dp, flip_by(z, slot)),
                            device_id_type=pl.DeviceIdType.MESH)
    targets = [(section, core_peer, z), (section, chip_peer, z)]
    targets += [(other, dp, flip_by(z, slot)) for slot in range(n)]
    for target in targets:
        pl.semaphore_signal(barrier, inc=1, device_id=target, device_id_type=pl.DeviceIdType.MESH)

    def remote(src, dst, send, recv, target):
        return pltpu.make_async_remote_copy(
            src_ref=src, dst_ref=dst, send_sem=send, recv_sem=recv,
            device_id=target, device_id_type=pl.DeviceIdType.MESH)

    own = pl.multiple_of(z * cols, cols)
    locals_ = [
        pltpu.make_async_copy(activ_hbm.at[0], activ, local_sem.at[0]),
        pltpu.make_async_copy(query_hbm.at[0], query, local_sem.at[1]),
        pltpu.make_async_copy(key_hbm.at[0], key, local_sem.at[2]),
        pltpu.make_async_copy(wv_hbm.at[0, pl.ds(own, cols), :], wv.at[0], local_sem.at[3]),
    ]
    pl.semaphore_wait(barrier, 2 * n + 1)

    pieces = [("v", 3, sub) for sub in range(V_SUB)]
    pieces += [("v", slot, sub) for sub in range(V_SUB) for slot in (2, 1)]
    n_value = len(pieces)
    pieces += [("o", slot, sub) for sub in range(O_SUB) for slot in (3, 2, 1)]
    pieces += [("o", 0, sub) for sub in range(O_SUB)]
    n_tensor = n_value + O_SUB * (n - 1)

    def v_at(slot, which, sub):
        rows = pl.ds(pl.multiple_of(which * quarter + sub * v_rows, v_rows), v_rows)
        return wv.at[slot, rows, :]

    def o_at(slot, which, sub):
        columns = pl.ds(pl.multiple_of(which * quarter + o_start[sub], unit), o_cols[sub])
        return wo.at[slot, :, columns]

    def copies(piece):
        kind, slot, sub = piece
        peer = flip_by(z, slot)
        if kind == "v":
            start = pl.multiple_of(peer * cols + dp * quarter + sub * v_rows, v_rows)
            source = wv_hbm.at[0, pl.ds(start, v_rows), :]
            at, send, recv, index, target = v_at, wv_send, wv_recv, slot - 1, (section, dp, peer)
        else:
            start = pl.multiple_of(peer * cols + dp * quarter + o_start[sub], unit)
            source = wo_hbm.at[0, :, pl.ds(start, o_cols[sub])]
            at, send, recv, index, target = o_at, wo_send, wo_recv, slot, (other, dp, peer)
        mine, far = at(slot, dp, sub), at(slot, chip_peer, sub)
        def sems(hop):
            return send.at[index, sub, hop], recv.at[index, sub, hop]
        return (
            remote(source, mine, *sems(0), target),
            remote(mine, mine, *sems(1), (section, core_peer, z)),
            remote(mine, mine, *sems(2), (section, chip_peer, z)),
            remote(far, far, *sems(3), (section, core_peer, z)),
        )

    plan = [copies(piece) for piece in pieces]
    for i in range(WINDOW):
        plan[i][0].start()
    for copy in locals_:
        copy.start()
    residual_copy = remote(activ_hbm.at[0], residual, residual_sem.at[0], residual_sem.at[1], (other, dp, z))
    for i in range(n_tensor, len(plan)):
        plan[i][0].start()
    residual_copy.start()

    def pass_on(i):
        plan[i][0].wait_recv()
        plan[i][2].start()
        plan[i][1].start()

    def relay(i):
        plan[i][2].wait_recv()
        plan[i][3].start()

    locals_[1].wait()
    locals_[2].wait()
    causal = lax.broadcasted_iota(jnp.int32, (LEN, LEN), 1) <= lax.broadcasted_iota(jnp.int32, (LEN, LEN), 0)
    scale = 1.0 / HEAD_SIZE**0.5
    heads = query.shape[1] // HEAD_SIZE
    blocks = [(start, head) for start in range(0, length, LEN) for head in range(heads)]
    for at, (start, head) in enumerate(blocks):
        rows, span = slice(start, start + LEN), slice(head * HEAD_SIZE, (head + 1) * HEAD_SIZE)
        scores = lax.dot_general(query[rows, span], key[rows, span], (((1,), (1,)), ((), ())),
                                 preferred_element_type=jnp.float32) * scale
        scores = jnp.where(causal, scores, -1e30)
        expo = jnp.exp(scores - jnp.max(scores, axis=-1, keepdims=True))
        probs[at] = (expo / jnp.sum(expo, axis=-1, keepdims=True)).astype(jnp.bfloat16)
    locals_[0].wait()
    locals_[3].wait()
    own_part[...] = jnp.dot(activ[...], wv[0], preferred_element_type=jnp.float32)

    near, across = flip_by(z, 1), flip_by(z, 2)
    value_copies = [
        remote(part_out.at[m], part_in.at[m], value_send.at[m], value_recv.at[m], (section, dp, to))
        for m, to in enumerate((near, across, near))]

    def send_value(slot):
        for i, (kind, at, _) in enumerate(pieces):
            if kind == "v" and at == slot:
                plan[i][1].wait_recv()
                plan[i][3].wait_recv()
        term = jnp.dot(activ[...], wv[slot], preferred_element_type=jnp.float32)
        if slot == 2:
            value_copies[0].wait_recv()
            term = term + part_in[0].astype(jnp.float32)
        part_out[3 - slot] = term.astype(jnp.bfloat16)
        value_copies[3 - slot].start()

    def advance(i):
        pass_on(i)
        if i + WINDOW < n_tensor:
            plan[i][0].wait_send()
            plan[i + WINDOW][0].start()

    for i in range(n_value):
        advance(i)
        if i > 0:
            relay(i - 1)
        if i == V_SUB + 1:
            send_value(3)
    relay(n_value - 1)
    send_value(2)
    send_value(1)

    def piece_range(sub):
        first = n_value + sub * (n - 1)
        return [n_tensor + sub] + list(range(first, first + n - 1))

    def bring(sub):
        batch = piece_range(sub)
        pass_on(batch[0])
        for before, i in zip(batch, batch[1:]):
            advance(i)
            relay(before)

    bring(0)
    value_copies[1].wait_recv()
    value_copies[2].wait_recv()
    total = own_part[...] + part_in[1].astype(jnp.float32) + part_in[2].astype(jnp.float32)
    values = total.astype(jnp.bfloat16)
    for at, (start, head) in enumerate(blocks):
        rows, span = slice(start, start + LEN), slice(head * HEAD_SIZE, (head + 1) * HEAD_SIZE)
        own_context[rows, span] = jnp.dot(
            probs[at], values[rows, span], preferred_element_type=jnp.float32).astype(jnp.bfloat16)

    routes = [(own_context, 2, (other, dp, across)), (own_context, 1, (other, dp, near)),
              (own_context, 0, (other, dp, z)), (context.at[2], 3, (section, dp, near))]
    context_copies = [
        remote(src, context.at[dst], context_send.at[m], context_recv.at[m], to)
        for m, (src, dst, to) in enumerate(routes)]
    for copy in context_copies[:3]:
        copy.start()
    relay(piece_range(0)[-1])
    bring(1)
    context_copies[0].wait_recv()
    context_copies[3].start()
    relay(piece_range(1)[-1])

    out_copies = []

    def chunk(sub, order):
        for i in piece_range(sub):
            if order == 1:
                plan[i][1].wait_recv()
            elif order == 3:
                plan[i][3].wait_recv()
        columns = pl.ds(pl.multiple_of(quarters[order] * quarter + o_start[sub], unit), o_cols[sub])
        total = residual[:, columns].astype(jnp.float32)
        for slot in range(n):
            total = total + jnp.dot(context[slot], wo[slot, :, columns],
                                    preferred_element_type=jnp.float32)
        result[:, columns] = total.astype(jnp.bfloat16)
        copy = pltpu.make_async_copy(result.at[:, columns], out_hbm.at[0, :, columns], out_sem.at[sub, order])
        copy.start()
        out_copies.append(copy)

    for sub in range(2, O_SUB):
        bring(sub)
        if sub == 2:
            residual_copy.wait_recv()
            for copy in context_copies[1:]:
                copy.wait_recv()
            for order in range(4):
                chunk(0, order)
        relay(piece_range(sub)[-1])
        for order in range(4):
            chunk(sub - 1, order)
    for order in range(4):
        chunk(O_SUB - 1, order)

    for i, piece in enumerate(plan):
        if not i + WINDOW < n_tensor:
            piece[0].wait_send()
        for copy in piece[1:]:
            copy.wait_send()
    for copy in value_copies + context_copies + [residual_copy]:
        copy.wait_send()
    for copy in out_copies:
        copy.wait()


def by_weights(n, inputs, queries, keys, w_value, w_out):
    length, cols = inputs.shape[1:]
    width = w_value.shape[2]
    bf16, dma = jnp.bfloat16, pltpu.SemaphoreType.DMA
    return pl.pallas_call(
        functools.partial(moving_weights, n),
        out_shape=jax.ShapeDtypeStruct(inputs.shape, bf16),
        in_specs=[pl.BlockSpec(memory_space=pl.ANY)] * 5,
        out_specs=pl.BlockSpec(memory_space=pl.ANY),
        scratch_shapes=[
            pltpu.VMEM((length, cols), bf16),
            pltpu.VMEM((length, cols), bf16),
            pltpu.VMEM((length, width), bf16),
            pltpu.VMEM((length, width), bf16),
            pltpu.VMEM((n, cols, width), bf16),
            pltpu.VMEM((n, width, cols), bf16),
            pltpu.VMEM((length // LEN * width // HEAD_SIZE, LEN, LEN), bf16),
            pltpu.VMEM((length, width), jnp.float32),
            pltpu.VMEM((n - 1, length, width), bf16),
            pltpu.VMEM((n - 1, length, width), bf16),
            pltpu.VMEM((length, width), bf16),
            pltpu.VMEM((n, length, width), bf16),
            pltpu.VMEM((length, cols), bf16),
            dma((4,)),
            dma((2,)),
            dma((n - 1, V_SUB, 4)),
            dma((n - 1, V_SUB, 4)),
            dma((n, O_SUB, 4)),
            dma((n, O_SUB, 4)),
            dma((n - 1,)),
            dma((n - 1,)),
            dma((n,)),
            dma((n,)),
            dma((O_SUB, 4)),
        ],
        compiler_params=pltpu.CompilerParams(
            collective_id=0, has_side_effects=True, vmem_limit_bytes=60 * 2**20),
        cost_estimate=pl.CostEstimate(
            flops=4 * length * cols * n * width, bytes_accessed=2 * 4 * n * cols * width,
            transcendentals=length * LEN * width // HEAD_SIZE),
        name="weights_to_activations",
    )(inputs, queries, keys, w_value, w_out)


def by_activations(inputs, queries, keys, w_value, w_out):
    activ = inputs[0]
    weight_v = w_value[0]
    weight_o = w_out[0]
    length = activ.shape[0]
    col_width = activ.shape[1]
    features_all = lax.all_gather(activ, "tensor", axis=1, tiled=True)
    values = jnp.dot(features_all, weight_v, preferred_element_type=jnp.float32)
    values = values.astype(jnp.bfloat16)
    heads_here = weight_v.shape[1] // HEAD_SIZE
    query_rows = queries[0].reshape(length // LEN, LEN, heads_here, HEAD_SIZE)
    key_rows = keys[0].reshape(length // LEN, LEN, heads_here, HEAD_SIZE)
    value_rows = values.reshape(length // LEN, LEN, heads_here, HEAD_SIZE)
    scores = jnp.einsum(
        "bqhd,bkhd->bhqk", query_rows, key_rows, preferred_element_type=jnp.float32
    ) / jnp.sqrt(jnp.float32(HEAD_SIZE))
    rows = lax.broadcasted_iota(jnp.int32, (LEN, LEN), 0)
    cols = lax.broadcasted_iota(jnp.int32, (LEN, LEN), 1)
    scores = jnp.where((cols <= rows)[None, None], scores, jnp.float32(-1e30))
    top = jnp.max(scores, axis=-1, keepdims=True)
    expo = jnp.exp(scores - top)
    probs = (expo / jnp.sum(expo, axis=-1, keepdims=True)).astype(jnp.bfloat16)
    context = jnp.einsum(
        "bhqk,bkhd->bqhd", probs, value_rows, preferred_element_type=jnp.float32
    ).astype(jnp.bfloat16)
    context = context.reshape(length, heads_here * HEAD_SIZE)
    partial_term = jnp.dot(context, weight_o, preferred_element_type=jnp.float32)
    total = lax.psum_scatter(
        partial_term.astype(jnp.bfloat16), "tensor", scatter_dimension=1, tiled=True)
    result = (total.astype(jnp.float32) + activ.astype(jnp.float32)).astype(jnp.bfloat16)
    size = lax.axis_size("section")
    return lax.ppermute(result, "section", [(i, i ^ 1) for i in range(size)])[None]


def solution(mesh):
    n = mesh.shape["tensor"]

    def on_device(inputs, queries, keys, w_value, w_out):
        length, cols = inputs.shape[1:]
        width = w_value.shape[2]
        weights_smaller = n * width <= mesh.shape["dp"] * length
        divides = (cols % (4 * 128 * O_UNITS) == 0 and cols % (4 * 16 * V_SUB) == 0
                   and length % LEN == 0 and n == GROUP and mesh.shape["dp"] == 4)
        if weights_smaller and divides:
            return by_weights(n, inputs, queries, keys, w_value, w_out)
        return by_activations(inputs, queries, keys, w_value, w_out)

    return jax.shard_map(
        on_device,
        mesh=mesh,
        in_specs=(
            P("section", "dp", "tensor"),
            P("section", "dp", "tensor"),
            P("section", "dp", "tensor"),
            P("section", None, "tensor"),
            P("section", "tensor", None),
        ),
        out_specs=P("section", "dp", "tensor"),
        check_vma=False,
    )
```

```python
import functools

import jax
import jax.numpy as jnp
from jax import lax
from jax.experimental import pallas as pl
from jax.experimental.pallas import tpu as pltpu
from jax.sharding import PartitionSpec as P

HEAD_SIZE = 128
LEN = 256
V_SUB = 3
O_SHARES = (2, 2, 1, 1)
O_SUB, O_UNITS = len(O_SHARES), sum(O_SHARES)
WINDOW = 4
O_EARLY = 2
O_WINDOW = 6
GROUP = 4


def flip(index, bit):
    step = 2**bit
    return index + step - 2 * step * lax.rem(index // step, 2)


def flip_by(index, mask):
    for bit in range(mask.bit_length()):
        if mask >> bit & 1:
            index = flip(index, bit)
    return index


def moving_weights(
    n,
    activ_hbm, query_hbm, key_hbm, wv_hbm, wo_hbm, out_hbm,
    activ, residual, query, key, wv, wo, probs, own_part, part_out, part_in, own_context, context, result,
    local_sem, residual_sem, wv_send, wv_recv, wo_send, wo_recv, value_send, value_recv, context_send, context_recv, out_sem,
):
    section = lax.axis_index("section")
    dp = lax.axis_index("dp")
    z = lax.axis_index("tensor")
    length, cols = activ.shape
    quarter = cols // 4
    v_rows = quarter // V_SUB
    unit = quarter // O_UNITS
    o_start = [sum(O_SHARES[:sub]) * unit for sub in range(O_SUB)]
    o_cols = [share * unit for share in O_SHARES]
    core_peer = flip(dp, 0)
    chip_peer = flip(dp, 1)
    diagonal = flip(core_peer, 1)
    quarters = (dp, core_peer, chip_peer, diagonal)
    other = flip(section, 0)

    barrier = pltpu.get_barrier_semaphore()
    for slot in range(1, n):
        pl.semaphore_signal(barrier, inc=1, device_id=(section, dp, flip_by(z, slot)),
                            device_id_type=pl.DeviceIdType.MESH)
    targets = [(section, core_peer, z), (section, chip_peer, z)]
    targets += [(other, dp, flip_by(z, slot)) for slot in range(n)]
    for target in targets:
        pl.semaphore_signal(barrier, inc=1, device_id=target, device_id_type=pl.DeviceIdType.MESH)

    def remote(src, dst, send, recv, target):
        return pltpu.make_async_remote_copy(
            src_ref=src, dst_ref=dst, send_sem=send, recv_sem=recv,
            device_id=target, device_id_type=pl.DeviceIdType.MESH)

    own = pl.multiple_of(z * cols, cols)
    locals_ = [
        pltpu.make_async_copy(activ_hbm.at[0], activ, local_sem.at[0]),
        pltpu.make_async_copy(query_hbm.at[0], query, local_sem.at[1]),
        pltpu.make_async_copy(key_hbm.at[0], key, local_sem.at[2]),
        pltpu.make_async_copy(wv_hbm.at[0, pl.ds(own, cols), :], wv.at[0], local_sem.at[3]),
    ]
    pl.semaphore_wait(barrier, 2 * n + 1)

    pieces = [("v", 3, sub) for sub in range(V_SUB)]
    pieces += [("v", slot, sub) for sub in range(V_SUB) for slot in (2, 1)]
    n_value = len(pieces)
    pieces += [("o", slot, sub) for sub in range(O_SUB) for slot in (3, 2, 1)]
    pieces += [("o", 0, sub) for sub in range(O_SUB)]
    n_tensor = n_value + O_SUB * (n - 1)

    def v_at(slot, which, sub):
        rows = pl.ds(pl.multiple_of(which * quarter + sub * v_rows, v_rows), v_rows)
        return wv.at[slot, rows, :]

    def o_at(slot, which, sub):
        columns = pl.ds(pl.multiple_of(which * quarter + o_start[sub], unit), o_cols[sub])
        return wo.at[slot, :, columns]

    def copies(piece):
        kind, slot, sub = piece
        peer = flip_by(z, slot)
        if kind == "v":
            start = pl.multiple_of(peer * cols + dp * quarter + sub * v_rows, v_rows)
            source = wv_hbm.at[0, pl.ds(start, v_rows), :]
            at, send, recv, index, target = v_at, wv_send, wv_recv, slot - 1, (section, dp, peer)
        else:
            start = pl.multiple_of(peer * cols + dp * quarter + o_start[sub], unit)
            source = wo_hbm.at[0, :, pl.ds(start, o_cols[sub])]
            at, send, recv, index, target = o_at, wo_send, wo_recv, slot, (other, dp, peer)
        mine, far = at(slot, dp, sub), at(slot, chip_peer, sub)
        def sems(hop):
            return send.at[index, sub, hop], recv.at[index, sub, hop]
        return (
            remote(source, mine, *sems(0), target),
            remote(mine, mine, *sems(1), (section, core_peer, z)),
            remote(mine, mine, *sems(2), (section, chip_peer, z)),
            remote(far, far, *sems(3), (section, core_peer, z)),
        )

    plan = [copies(piece) for piece in pieces]
    for i in range(WINDOW):
        plan[i][0].start()
    for copy in locals_:
        copy.start()
    residual_copy = remote(activ_hbm.at[0], residual, residual_sem.at[0], residual_sem.at[1], (other, dp, z))
    for i in range(n_tensor, len(plan)):
        plan[i][0].start()

    def pass_on(i):
        plan[i][0].wait_recv()
        plan[i][2].start()
        plan[i][1].start()

    def relay(i):
        plan[i][2].wait_recv()
        plan[i][3].start()

    locals_[1].wait()
    locals_[2].wait()
    causal = lax.broadcasted_iota(jnp.int32, (LEN, LEN), 1) <= lax.broadcasted_iota(jnp.int32, (LEN, LEN), 0)
    scale = 1.0 / HEAD_SIZE**0.5
    heads = query.shape[1] // HEAD_SIZE
    blocks = [(start, head) for start in range(0, length, LEN) for head in range(heads)]
    for at, (start, head) in enumerate(blocks):
        rows, span = slice(start, start + LEN), slice(head * HEAD_SIZE, (head + 1) * HEAD_SIZE)
        scores = lax.dot_general(query[rows, span], key[rows, span], (((1,), (1,)), ((), ())),
                                 preferred_element_type=jnp.float32) * scale
        scores = jnp.where(causal, scores, -1e30)
        expo = jnp.exp(scores - jnp.max(scores, axis=-1, keepdims=True))
        probs[at] = (expo / jnp.sum(expo, axis=-1, keepdims=True)).astype(jnp.bfloat16)
    locals_[0].wait()
    locals_[3].wait()
    own_part[...] = jnp.dot(activ[...], wv[0], preferred_element_type=jnp.float32)

    near, across = flip_by(z, 1), flip_by(z, 2)
    value_copies = [
        remote(part_out.at[m], part_in.at[m], value_send.at[m], value_recv.at[m], (section, dp, to))
        for m, to in enumerate((near, across, near))]

    def send_value(slot):
        for i, (kind, at, _) in enumerate(pieces):
            if kind == "v" and at == slot:
                plan[i][1].wait_recv()
                plan[i][3].wait_recv()
        term = jnp.dot(activ[...], wv[slot], preferred_element_type=jnp.float32)
        if slot == 2:
            value_copies[0].wait_recv()
            term = term + part_in[0].astype(jnp.float32)
        part_out[3 - slot] = term.astype(jnp.bfloat16)
        value_copies[3 - slot].start()

    started = WINDOW
    sent = set()

    def advance(i):
        nonlocal started
        pass_on(i)
        if started < n_tensor:
            plan[i][0].wait_send()
            sent.add(i)
        ahead = i + 1 + (WINDOW if i + 1 < n_value else O_WINDOW)
        while started < min(ahead, n_tensor):
            plan[started][0].start()
            started += 1

    for i in range(n_value):
        advance(i)
        if i == V_SUB:
            residual_copy.start()
        if i > V_SUB and i - V_SUB - 1 < O_EARLY:
            pass_on(n_tensor + i - V_SUB - 1)
        if i > 0:
            relay(i - 1)
        if i == V_SUB + 1:
            send_value(3)
    relay(n_value - 1)
    send_value(2)
    send_value(1)

    def piece_range(sub):
        first = n_value + sub * (n - 1)
        return [n_tensor + sub] + list(range(first, first + n - 1))

    def bring(sub, between=None):
        batch = piece_range(sub)
        if sub >= O_EARLY:
            pass_on(batch[0])
        for at, (before, i) in enumerate(zip(batch, batch[1:])):
            advance(i)
            relay(before)
            if between is not None:
                between(at)

    bring(0)
    value_copies[1].wait_recv()
    value_copies[2].wait_recv()
    total = own_part[...] + part_in[1].astype(jnp.float32) + part_in[2].astype(jnp.float32)
    values = total.astype(jnp.bfloat16)
    for at, (start, head) in enumerate(blocks):
        rows, span = slice(start, start + LEN), slice(head * HEAD_SIZE, (head + 1) * HEAD_SIZE)
        own_context[rows, span] = jnp.dot(
            probs[at], values[rows, span], preferred_element_type=jnp.float32).astype(jnp.bfloat16)

    routes = [(own_context, 2, (other, dp, across)), (own_context, 1, (other, dp, near)),
              (own_context, 0, (other, dp, z)), (context.at[2], 3, (section, dp, near))]
    context_copies = [
        remote(src, context.at[dst], context_send.at[m], context_recv.at[m], to)
        for m, (src, dst, to) in enumerate(routes)]
    for copy in context_copies[:3]:
        copy.start()
    relay(piece_range(0)[-1])
    bring(1)
    context_copies[0].wait_recv()
    context_copies[3].start()
    relay(piece_range(1)[-1])

    out_copies = []

    def chunk(sub, order):
        for i in piece_range(sub):
            if order == 1:
                plan[i][1].wait_recv()
            elif order == 3:
                plan[i][3].wait_recv()
        columns = pl.ds(pl.multiple_of(quarters[order] * quarter + o_start[sub], unit), o_cols[sub])
        total = residual[:, columns].astype(jnp.float32)
        for slot in range(n):
            total = total + jnp.dot(context[slot], wo[slot, :, columns],
                                    preferred_element_type=jnp.float32)
        result[:, columns] = total.astype(jnp.bfloat16)
        copy = pltpu.make_async_copy(result.at[:, columns], out_hbm.at[0, :, columns], out_sem.at[sub, order])
        copy.start()
        out_copies.append(copy)

    residual_copy.wait_recv()
    for copy in context_copies[1:]:
        copy.wait_recv()
    for order in range(4):
        chunk(0, order)
    for sub in range(2, O_SUB):
        def earlier(at):
            for order in {0: (0, 1), 1: (2, 3)}.get(at, ()):
                chunk(sub - 1, order)
        bring(sub, earlier)
        relay(piece_range(sub)[-1])
    for order in range(4):
        chunk(O_SUB - 1, order)

    for i, piece in enumerate(plan):
        if i not in sent:
            piece[0].wait_send()
        for copy in piece[1:]:
            copy.wait_send()
    for copy in value_copies + context_copies + [residual_copy]:
        copy.wait_send()
    for copy in out_copies:
        copy.wait()


def by_weights(n, inputs, queries, keys, w_value, w_out):
    length, cols = inputs.shape[1:]
    width = w_value.shape[2]
    bf16, dma = jnp.bfloat16, pltpu.SemaphoreType.DMA
    return pl.pallas_call(
        functools.partial(moving_weights, n),
        out_shape=jax.ShapeDtypeStruct(inputs.shape, bf16),
        in_specs=[pl.BlockSpec(memory_space=pl.ANY)] * 5,
        out_specs=pl.BlockSpec(memory_space=pl.ANY),
        scratch_shapes=[
            pltpu.VMEM((length, cols), bf16),
            pltpu.VMEM((length, cols), bf16),
            pltpu.VMEM((length, width), bf16),
            pltpu.VMEM((length, width), bf16),
            pltpu.VMEM((n, cols, width), bf16),
            pltpu.VMEM((n, width, cols), bf16),
            pltpu.VMEM((length // LEN * width // HEAD_SIZE, LEN, LEN), bf16),
            pltpu.VMEM((length, width), jnp.float32),
            pltpu.VMEM((n - 1, length, width), bf16),
            pltpu.VMEM((n - 1, length, width), bf16),
            pltpu.VMEM((length, width), bf16),
            pltpu.VMEM((n, length, width), bf16),
            pltpu.VMEM((length, cols), bf16),
            dma((4,)),
            dma((2,)),
            dma((n - 1, V_SUB, 4)),
            dma((n - 1, V_SUB, 4)),
            dma((n, O_SUB, 4)),
            dma((n, O_SUB, 4)),
            dma((n - 1,)),
            dma((n - 1,)),
            dma((n,)),
            dma((n,)),
            dma((O_SUB, 4)),
        ],
        compiler_params=pltpu.CompilerParams(
            collective_id=0, has_side_effects=True, vmem_limit_bytes=60 * 2**20),
        cost_estimate=pl.CostEstimate(
            flops=4 * length * cols * n * width, bytes_accessed=2 * 4 * n * cols * width,
            transcendentals=length * LEN * width // HEAD_SIZE),
        name="weights_to_activations",
    )(inputs, queries, keys, w_value, w_out)


def by_activations(inputs, queries, keys, w_value, w_out):
    activ = inputs[0]
    weight_v = w_value[0]
    weight_o = w_out[0]
    length = activ.shape[0]
    col_width = activ.shape[1]
    features_all = lax.all_gather(activ, "tensor", axis=1, tiled=True)
    values = jnp.dot(features_all, weight_v, preferred_element_type=jnp.float32)
    values = values.astype(jnp.bfloat16)
    heads_here = weight_v.shape[1] // HEAD_SIZE
    query_rows = queries[0].reshape(length // LEN, LEN, heads_here, HEAD_SIZE)
    key_rows = keys[0].reshape(length // LEN, LEN, heads_here, HEAD_SIZE)
    value_rows = values.reshape(length // LEN, LEN, heads_here, HEAD_SIZE)
    scores = jnp.einsum(
        "bqhd,bkhd->bhqk", query_rows, key_rows, preferred_element_type=jnp.float32
    ) / jnp.sqrt(jnp.float32(HEAD_SIZE))
    rows = lax.broadcasted_iota(jnp.int32, (LEN, LEN), 0)
    cols = lax.broadcasted_iota(jnp.int32, (LEN, LEN), 1)
    scores = jnp.where((cols <= rows)[None, None], scores, jnp.float32(-1e30))
    top = jnp.max(scores, axis=-1, keepdims=True)
    expo = jnp.exp(scores - top)
    probs = (expo / jnp.sum(expo, axis=-1, keepdims=True)).astype(jnp.bfloat16)
    context = jnp.einsum(
        "bhqk,bkhd->bqhd", probs, value_rows, preferred_element_type=jnp.float32
    ).astype(jnp.bfloat16)
    context = context.reshape(length, heads_here * HEAD_SIZE)
    partial_term = jnp.dot(context, weight_o, preferred_element_type=jnp.float32)
    total = lax.psum_scatter(
        partial_term.astype(jnp.bfloat16), "tensor", scatter_dimension=1, tiled=True)
    result = (total.astype(jnp.float32) + activ.astype(jnp.float32)).astype(jnp.bfloat16)
    size = lax.axis_size("section")
    return lax.ppermute(result, "section", [(i, i ^ 1) for i in range(size)])[None]


def solution(mesh):
    n = mesh.shape["tensor"]

    def on_device(inputs, queries, keys, w_value, w_out):
        length, cols = inputs.shape[1:]
        width = w_value.shape[2]
        weights_smaller = n * width <= mesh.shape["dp"] * length
        divides = (cols % (4 * 128 * O_UNITS) == 0 and cols % (4 * 16 * V_SUB) == 0
                   and length % LEN == 0 and n == GROUP and mesh.shape["dp"] == 4)
        if weights_smaller and divides:
            return by_weights(n, inputs, queries, keys, w_value, w_out)
        return by_activations(inputs, queries, keys, w_value, w_out)

    return jax.shard_map(
        on_device,
        mesh=mesh,
        in_specs=(
            P("section", "dp", "tensor"),
            P("section", "dp", "tensor"),
            P("section", "dp", "tensor"),
            P("section", None, "tensor"),
            P("section", "tensor", None),
        ),
        out_specs=P("section", "dp", "tensor"),
        check_vma=False,
    )
```

```python
import functools

import jax
import jax.numpy as jnp
from jax import lax
from jax.experimental import pallas as pl
from jax.experimental.pallas import tpu as pltpu
from jax.sharding import PartitionSpec as P

HEAD_SIZE = 128
LEN = 256
V_SUB = 3
O_SHARES = (2, 2, 1, 1)
O_SUB, O_UNITS = len(O_SHARES), sum(O_SHARES)
WINDOW = 4
O_WINDOW = 3
GROUP = 4


def flip(index, bit):
    step = 2**bit
    return index + step - 2 * step * lax.rem(index // step, 2)


def flip_by(index, mask):
    for bit in range(mask.bit_length()):
        if mask >> bit & 1:
            index = flip(index, bit)
    return index


def moving_weights(
    n,
    activ_hbm, query_hbm, key_hbm, wv_hbm, wo_hbm, out_hbm,
    activ, residual, query, key, wv, wo, probs, own_part, part_out, part_in, own_context, context, result,
    local_sem, residual_sem, wv_send, wv_recv, wo_send, wo_recv, value_send, value_recv, context_send, context_recv, out_sem,
):
    section = lax.axis_index("section")
    dp = lax.axis_index("dp")
    z = lax.axis_index("tensor")
    length, cols = activ.shape
    quarter = cols // 4
    v_rows = quarter // V_SUB
    unit = quarter // O_UNITS
    o_start = [sum(O_SHARES[:sub]) * unit for sub in range(O_SUB)]
    o_cols = [share * unit for share in O_SHARES]
    core_peer = flip(dp, 0)
    chip_peer = flip(dp, 1)
    diagonal = flip(core_peer, 1)
    quarters = (dp, core_peer, chip_peer, diagonal)
    other = flip(section, 0)

    barrier = pltpu.get_barrier_semaphore()
    for slot in range(1, n):
        pl.semaphore_signal(barrier, inc=1, device_id=(section, dp, flip_by(z, slot)),
                            device_id_type=pl.DeviceIdType.MESH)
    targets = [(section, core_peer, z), (section, chip_peer, z)]
    targets += [(other, dp, flip_by(z, slot)) for slot in range(n)]
    for target in targets:
        pl.semaphore_signal(barrier, inc=1, device_id=target, device_id_type=pl.DeviceIdType.MESH)

    def remote(src, dst, send, recv, target):
        return pltpu.make_async_remote_copy(
            src_ref=src, dst_ref=dst, send_sem=send, recv_sem=recv,
            device_id=target, device_id_type=pl.DeviceIdType.MESH)

    own = pl.multiple_of(z * cols, cols)
    locals_ = [
        pltpu.make_async_copy(activ_hbm.at[0], activ, local_sem.at[0]),
        pltpu.make_async_copy(query_hbm.at[0], query, local_sem.at[1]),
        pltpu.make_async_copy(key_hbm.at[0], key, local_sem.at[2]),
        pltpu.make_async_copy(wv_hbm.at[0, pl.ds(own, cols), :], wv.at[0], local_sem.at[3]),
    ]
    pl.semaphore_wait(barrier, 2 * n + 1)

    pieces = [("v", 3, sub) for sub in range(V_SUB)]
    pieces += [("v", slot, sub) for sub in range(V_SUB) for slot in (2, 1)]
    n_value = len(pieces)
    pieces += [("o", slot, sub) for sub in range(O_SUB) for slot in (3, 2, 1)]
    pieces += [("o", 0, sub) for sub in range(O_SUB)]
    n_tensor = n_value + O_SUB * (n - 1)

    def v_at(slot, which, sub):
        rows = pl.ds(pl.multiple_of(which * quarter + sub * v_rows, v_rows), v_rows)
        return wv.at[slot, rows, :]

    def o_at(slot, which, sub):
        columns = pl.ds(pl.multiple_of(which * quarter + o_start[sub], unit), o_cols[sub])
        return wo.at[slot, :, columns]

    def copies(piece):
        kind, slot, sub = piece
        peer = flip_by(z, slot)
        if kind == "v":
            start = pl.multiple_of(peer * cols + dp * quarter + sub * v_rows, v_rows)
            source = wv_hbm.at[0, pl.ds(start, v_rows), :]
            at, send, recv, index, target = v_at, wv_send, wv_recv, slot - 1, (section, dp, peer)
        else:
            start = pl.multiple_of(peer * cols + dp * quarter + o_start[sub], unit)
            source = wo_hbm.at[0, :, pl.ds(start, o_cols[sub])]
            at, send, recv, index, target = o_at, wo_send, wo_recv, slot, (other, dp, peer)
        mine, far = at(slot, dp, sub), at(slot, chip_peer, sub)
        def sems(hop):
            return send.at[index, sub, hop], recv.at[index, sub, hop]
        return (
            remote(source, mine, *sems(0), target),
            remote(mine, mine, *sems(1), (section, core_peer, z)),
            remote(mine, mine, *sems(2), (section, chip_peer, z)),
            remote(far, far, *sems(3), (section, core_peer, z)),
        )

    plan = [copies(piece) for piece in pieces]
    for i in range(WINDOW):
        plan[i][0].start()
    for copy in locals_:
        copy.start()
    residual_copy = remote(activ_hbm.at[0], residual, residual_sem.at[0], residual_sem.at[1], (other, dp, z))
    for i in range(n_tensor, len(plan)):
        plan[i][0].start()
    residual_copy.start()

    def pass_on(i):
        plan[i][0].wait_recv()
        plan[i][2].start()
        plan[i][1].start()

    def relay(i):
        plan[i][2].wait_recv()
        plan[i][3].start()

    locals_[1].wait()
    locals_[2].wait()
    causal = lax.broadcasted_iota(jnp.int32, (LEN, LEN), 1) <= lax.broadcasted_iota(jnp.int32, (LEN, LEN), 0)
    scale = 1.0 / HEAD_SIZE**0.5
    heads = query.shape[1] // HEAD_SIZE
    blocks = [(start, head) for start in range(0, length, LEN) for head in range(heads)]
    for at, (start, head) in enumerate(blocks):
        rows, span = slice(start, start + LEN), slice(head * HEAD_SIZE, (head + 1) * HEAD_SIZE)
        scores = lax.dot_general(query[rows, span], key[rows, span], (((1,), (1,)), ((), ())),
                                 preferred_element_type=jnp.float32) * scale
        scores = jnp.where(causal, scores, -1e30)
        expo = jnp.exp(scores - jnp.max(scores, axis=-1, keepdims=True))
        probs[at] = (expo / jnp.sum(expo, axis=-1, keepdims=True)).astype(jnp.bfloat16)
    locals_[0].wait()
    locals_[3].wait()
    own_part[...] = jnp.dot(activ[...], wv[0], preferred_element_type=jnp.float32)

    near, across = flip_by(z, 1), flip_by(z, 2)
    value_copies = [
        remote(part_out.at[m], part_in.at[m], value_send.at[m], value_recv.at[m], (section, dp, to))
        for m, to in enumerate((near, across, near))]

    def send_value(slot):
        for i, (kind, at, _) in enumerate(pieces):
            if kind == "v" and at == slot:
                plan[i][1].wait_recv()
                plan[i][3].wait_recv()
        term = jnp.dot(activ[...], wv[slot], preferred_element_type=jnp.float32)
        if slot == 2:
            value_copies[0].wait_recv()
            term = term + part_in[0].astype(jnp.float32)
        part_out[3 - slot] = term.astype(jnp.bfloat16)
        value_copies[3 - slot].start()

    started = WINDOW
    sent = set()

    def advance(i):
        nonlocal started
        pass_on(i)
        if started < n_tensor:
            plan[i][0].wait_send()
            sent.add(i)
        ahead = i + 1 + (WINDOW if i + 1 < n_value else O_WINDOW)
        while started < min(ahead, n_tensor):
            plan[started][0].start()
            started += 1

    for i in range(n_value):
        advance(i)
        if i > 0:
            relay(i - 1)
        if i == V_SUB + 1:
            send_value(3)
    relay(n_value - 1)
    send_value(2)
    send_value(1)

    def piece_range(sub):
        first = n_value + sub * (n - 1)
        return [n_tensor + sub] + list(range(first, first + n - 1))

    def bring(sub, between=None):
        batch = piece_range(sub)
        pass_on(batch[0])
        for at, (before, i) in enumerate(zip(batch, batch[1:])):
            advance(i)
            relay(before)
            if between is not None:
                between(at)

    bring(0)
    value_copies[1].wait_recv()
    value_copies[2].wait_recv()
    total = own_part[...] + part_in[1].astype(jnp.float32) + part_in[2].astype(jnp.float32)
    values = total.astype(jnp.bfloat16)
    for at, (start, head) in enumerate(blocks):
        rows, span = slice(start, start + LEN), slice(head * HEAD_SIZE, (head + 1) * HEAD_SIZE)
        own_context[rows, span] = jnp.dot(
            probs[at], values[rows, span], preferred_element_type=jnp.float32).astype(jnp.bfloat16)

    routes = [(own_context, 2, (other, dp, across)), (own_context, 1, (other, dp, near)),
              (own_context, 0, (other, dp, z)), (context.at[2], 3, (section, dp, near))]
    context_copies = [
        remote(src, context.at[dst], context_send.at[m], context_recv.at[m], to)
        for m, (src, dst, to) in enumerate(routes)]
    for copy in context_copies[:3]:
        copy.start()
    relay(piece_range(0)[-1])
    bring(1)
    context_copies[0].wait_recv()
    context_copies[3].start()
    relay(piece_range(1)[-1])

    out_copies = []

    def chunk(sub, order):
        for i in piece_range(sub):
            if order == 1:
                plan[i][1].wait_recv()
            elif order == 3:
                plan[i][3].wait_recv()
        columns = pl.ds(pl.multiple_of(quarters[order] * quarter + o_start[sub], unit), o_cols[sub])
        total = residual[:, columns].astype(jnp.float32)
        for slot in range(n):
            total = total + jnp.dot(context[slot], wo[slot, :, columns],
                                    preferred_element_type=jnp.float32)
        result[:, columns] = total.astype(jnp.bfloat16)
        copy = pltpu.make_async_copy(result.at[:, columns], out_hbm.at[0, :, columns], out_sem.at[sub, order])
        copy.start()
        out_copies.append(copy)

    residual_copy.wait_recv()
    for copy in context_copies[1:]:
        copy.wait_recv()
    for order in range(4):
        chunk(0, order)
    for sub in range(2, O_SUB):
        def earlier(at):
            for order in {0: (0, 1), 1: (2, 3)}.get(at, ()):
                chunk(sub - 1, order)
        bring(sub, earlier)
        relay(piece_range(sub)[-1])
    for order in range(4):
        chunk(O_SUB - 1, order)

    for i, piece in enumerate(plan):
        if i not in sent:
            piece[0].wait_send()
        for copy in piece[1:]:
            copy.wait_send()
    for copy in value_copies + context_copies + [residual_copy]:
        copy.wait_send()
    for copy in out_copies:
        copy.wait()


def by_weights(n, inputs, queries, keys, w_value, w_out):
    length, cols = inputs.shape[1:]
    width = w_value.shape[2]
    bf16, dma = jnp.bfloat16, pltpu.SemaphoreType.DMA
    return pl.pallas_call(
        functools.partial(moving_weights, n),
        out_shape=jax.ShapeDtypeStruct(inputs.shape, bf16),
        in_specs=[pl.BlockSpec(memory_space=pl.ANY)] * 5,
        out_specs=pl.BlockSpec(memory_space=pl.ANY),
        scratch_shapes=[
            pltpu.VMEM((length, cols), bf16),
            pltpu.VMEM((length, cols), bf16),
            pltpu.VMEM((length, width), bf16),
            pltpu.VMEM((length, width), bf16),
            pltpu.VMEM((n, cols, width), bf16),
            pltpu.VMEM((n, width, cols), bf16),
            pltpu.VMEM((length // LEN * width // HEAD_SIZE, LEN, LEN), bf16),
            pltpu.VMEM((length, width), jnp.float32),
            pltpu.VMEM((n - 1, length, width), bf16),
            pltpu.VMEM((n - 1, length, width), bf16),
            pltpu.VMEM((length, width), bf16),
            pltpu.VMEM((n, length, width), bf16),
            pltpu.VMEM((length, cols), bf16),
            dma((4,)),
            dma((2,)),
            dma((n - 1, V_SUB, 4)),
            dma((n - 1, V_SUB, 4)),
            dma((n, O_SUB, 4)),
            dma((n, O_SUB, 4)),
            dma((n - 1,)),
            dma((n - 1,)),
            dma((n,)),
            dma((n,)),
            dma((O_SUB, 4)),
        ],
        compiler_params=pltpu.CompilerParams(
            collective_id=0, has_side_effects=True, vmem_limit_bytes=60 * 2**20),
        cost_estimate=pl.CostEstimate(
            flops=4 * length * cols * n * width, bytes_accessed=2 * 4 * n * cols * width,
            transcendentals=length * LEN * width // HEAD_SIZE),
        name="weights_to_activations",
    )(inputs, queries, keys, w_value, w_out)


def by_activations(inputs, queries, keys, w_value, w_out):
    activ = inputs[0]
    weight_v = w_value[0]
    weight_o = w_out[0]
    length = activ.shape[0]
    col_width = activ.shape[1]
    features_all = lax.all_gather(activ, "tensor", axis=1, tiled=True)
    values = jnp.dot(features_all, weight_v, preferred_element_type=jnp.float32)
    values = values.astype(jnp.bfloat16)
    heads_here = weight_v.shape[1] // HEAD_SIZE
    query_rows = queries[0].reshape(length // LEN, LEN, heads_here, HEAD_SIZE)
    key_rows = keys[0].reshape(length // LEN, LEN, heads_here, HEAD_SIZE)
    value_rows = values.reshape(length // LEN, LEN, heads_here, HEAD_SIZE)
    scores = jnp.einsum(
        "bqhd,bkhd->bhqk", query_rows, key_rows, preferred_element_type=jnp.float32
    ) / jnp.sqrt(jnp.float32(HEAD_SIZE))
    rows = lax.broadcasted_iota(jnp.int32, (LEN, LEN), 0)
    cols = lax.broadcasted_iota(jnp.int32, (LEN, LEN), 1)
    scores = jnp.where((cols <= rows)[None, None], scores, jnp.float32(-1e30))
    top = jnp.max(scores, axis=-1, keepdims=True)
    expo = jnp.exp(scores - top)
    probs = (expo / jnp.sum(expo, axis=-1, keepdims=True)).astype(jnp.bfloat16)
    context = jnp.einsum(
        "bhqk,bkhd->bqhd", probs, value_rows, preferred_element_type=jnp.float32
    ).astype(jnp.bfloat16)
    context = context.reshape(length, heads_here * HEAD_SIZE)
    partial_term = jnp.dot(context, weight_o, preferred_element_type=jnp.float32)
    total = lax.psum_scatter(
        partial_term.astype(jnp.bfloat16), "tensor", scatter_dimension=1, tiled=True)
    result = (total.astype(jnp.float32) + activ.astype(jnp.float32)).astype(jnp.bfloat16)
    size = lax.axis_size("section")
    return lax.ppermute(result, "section", [(i, i ^ 1) for i in range(size)])[None]


def solution(mesh):
    n = mesh.shape["tensor"]

    def on_device(inputs, queries, keys, w_value, w_out):
        length, cols = inputs.shape[1:]
        width = w_value.shape[2]
        weights_smaller = n * width <= mesh.shape["dp"] * length
        divides = (cols % (4 * 128 * O_UNITS) == 0 and cols % (4 * 16 * V_SUB) == 0
                   and length % LEN == 0 and n == GROUP and mesh.shape["dp"] == 4)
        if weights_smaller and divides:
            return by_weights(n, inputs, queries, keys, w_value, w_out)
        return by_activations(inputs, queries, keys, w_value, w_out)

    return jax.shard_map(
        on_device,
        mesh=mesh,
        in_specs=(
            P("section", "dp", "tensor"),
            P("section", "dp", "tensor"),
            P("section", "dp", "tensor"),
            P("section", None, "tensor"),
            P("section", "tensor", None),
        ),
        out_specs=P("section", "dp", "tensor"),
        check_vma=False,
    )
```

```python
import functools

import jax
import jax.numpy as jnp
from jax import lax
from jax.experimental import pallas as pl
from jax.experimental.pallas import tpu as pltpu
from jax.sharding import PartitionSpec as P

HEAD_SIZE = 128
LEN = 256
V_SUB = 3
O_SHARES = (2, 2, 1, 1)
O_SUB, O_UNITS = len(O_SHARES), sum(O_SHARES)
WINDOW = 4
O_WINDOW = 6
GROUP = 4


def flip(index, bit):
    step = 2**bit
    return index + step - 2 * step * lax.rem(index // step, 2)


def flip_by(index, mask):
    for bit in range(mask.bit_length()):
        if mask >> bit & 1:
            index = flip(index, bit)
    return index


def moving_weights(
    n,
    activ_hbm, query_hbm, key_hbm, wv_hbm, wo_hbm, out_hbm,
    activ, residual, query, key, wv, wo, probs, own_part, part_out, part_in, own_context, context, result,
    local_sem, residual_sem, wv_send, wv_recv, wo_send, wo_recv, value_send, value_recv, context_send, context_recv, out_sem,
):
    section = lax.axis_index("section")
    dp = lax.axis_index("dp")
    z = lax.axis_index("tensor")
    length, cols = activ.shape
    quarter = cols // 4
    v_rows = quarter // V_SUB
    unit = quarter // O_UNITS
    o_start = [sum(O_SHARES[:sub]) * unit for sub in range(O_SUB)]
    o_cols = [share * unit for share in O_SHARES]
    core_peer = flip(dp, 0)
    chip_peer = flip(dp, 1)
    diagonal = flip(core_peer, 1)
    quarters = (dp, core_peer, chip_peer, diagonal)
    other = flip(section, 0)

    barrier = pltpu.get_barrier_semaphore()
    for slot in range(1, n):
        pl.semaphore_signal(barrier, inc=1, device_id=(section, dp, flip_by(z, slot)),
                            device_id_type=pl.DeviceIdType.MESH)
    targets = [(section, core_peer, z), (section, chip_peer, z)]
    targets += [(other, dp, flip_by(z, slot)) for slot in range(n)]
    for target in targets:
        pl.semaphore_signal(barrier, inc=1, device_id=target, device_id_type=pl.DeviceIdType.MESH)

    def remote(src, dst, send, recv, target):
        return pltpu.make_async_remote_copy(
            src_ref=src, dst_ref=dst, send_sem=send, recv_sem=recv,
            device_id=target, device_id_type=pl.DeviceIdType.MESH)

    own = pl.multiple_of(z * cols, cols)
    locals_ = [
        pltpu.make_async_copy(activ_hbm.at[0], activ, local_sem.at[0]),
        pltpu.make_async_copy(query_hbm.at[0], query, local_sem.at[1]),
        pltpu.make_async_copy(key_hbm.at[0], key, local_sem.at[2]),
        pltpu.make_async_copy(wv_hbm.at[0, pl.ds(own, cols), :], wv.at[0], local_sem.at[3]),
    ]
    pl.semaphore_wait(barrier, 2 * n + 1)

    pieces = [("v", 3, sub) for sub in range(V_SUB)]
    pieces += [("v", slot, sub) for sub in range(V_SUB) for slot in (2, 1)]
    n_value = len(pieces)
    pieces += [("o", slot, sub) for sub in range(O_SUB) for slot in (3, 2, 1)]
    pieces += [("o", 0, sub) for sub in range(O_SUB)]
    n_tensor = n_value + O_SUB * (n - 1)

    def v_at(slot, which, sub):
        rows = pl.ds(pl.multiple_of(which * quarter + sub * v_rows, v_rows), v_rows)
        return wv.at[slot, rows, :]

    def o_at(slot, which, sub):
        columns = pl.ds(pl.multiple_of(which * quarter + o_start[sub], unit), o_cols[sub])
        return wo.at[slot, :, columns]

    def copies(piece):
        kind, slot, sub = piece
        peer = flip_by(z, slot)
        if kind == "v":
            start = pl.multiple_of(peer * cols + dp * quarter + sub * v_rows, v_rows)
            source = wv_hbm.at[0, pl.ds(start, v_rows), :]
            at, send, recv, index, target = v_at, wv_send, wv_recv, slot - 1, (section, dp, peer)
        else:
            start = pl.multiple_of(peer * cols + dp * quarter + o_start[sub], unit)
            source = wo_hbm.at[0, :, pl.ds(start, o_cols[sub])]
            at, send, recv, index, target = o_at, wo_send, wo_recv, slot, (other, dp, peer)
        mine, far = at(slot, dp, sub), at(slot, chip_peer, sub)
        def sems(hop):
            return send.at[index, sub, hop], recv.at[index, sub, hop]
        return (
            remote(source, mine, *sems(0), target),
            remote(mine, mine, *sems(1), (section, core_peer, z)),
            remote(mine, mine, *sems(2), (section, chip_peer, z)),
            remote(far, far, *sems(3), (section, core_peer, z)),
        )

    plan = [copies(piece) for piece in pieces]
    for i in range(WINDOW):
        plan[i][0].start()
    for copy in locals_:
        copy.start()
    residual_copy = remote(activ_hbm.at[0], residual, residual_sem.at[0], residual_sem.at[1], (other, dp, z))
    for i in range(n_tensor, len(plan)):
        plan[i][0].start()
    residual_copy.start()

    def pass_on(i):
        plan[i][0].wait_recv()
        plan[i][2].start()
        plan[i][1].start()

    def relay(i):
        plan[i][2].wait_recv()
        plan[i][3].start()

    locals_[1].wait()
    locals_[2].wait()
    causal = lax.broadcasted_iota(jnp.int32, (LEN, LEN), 1) <= lax.broadcasted_iota(jnp.int32, (LEN, LEN), 0)
    scale = 1.0 / HEAD_SIZE**0.5
    heads = query.shape[1] // HEAD_SIZE
    blocks = [(start, head) for start in range(0, length, LEN) for head in range(heads)]
    for at, (start, head) in enumerate(blocks):
        rows, span = slice(start, start + LEN), slice(head * HEAD_SIZE, (head + 1) * HEAD_SIZE)
        scores = lax.dot_general(query[rows, span], key[rows, span], (((1,), (1,)), ((), ())),
                                 preferred_element_type=jnp.float32) * scale
        scores = jnp.where(causal, scores, -1e30)
        expo = jnp.exp(scores - jnp.max(scores, axis=-1, keepdims=True))
        probs[at] = (expo / jnp.sum(expo, axis=-1, keepdims=True)).astype(jnp.bfloat16)
    locals_[0].wait()
    locals_[3].wait()
    own_part[...] = jnp.dot(activ[...], wv[0], preferred_element_type=jnp.float32)

    near, across = flip_by(z, 1), flip_by(z, 2)
    value_copies = [
        remote(part_out.at[m], part_in.at[m], value_send.at[m], value_recv.at[m], (section, dp, to))
        for m, to in enumerate((near, across, near))]

    def send_value(slot):
        for i, (kind, at, _) in enumerate(pieces):
            if kind == "v" and at == slot:
                plan[i][1].wait_recv()
                plan[i][3].wait_recv()
        term = jnp.dot(activ[...], wv[slot], preferred_element_type=jnp.float32)
        if slot == 2:
            value_copies[0].wait_recv()
            term = term + part_in[0].astype(jnp.float32)
        part_out[3 - slot] = term.astype(jnp.bfloat16)
        value_copies[3 - slot].start()

    started = WINDOW
    sent = set()

    def advance(i):
        nonlocal started
        pass_on(i)
        if started < n_tensor:
            plan[i][0].wait_send()
            sent.add(i)
        ahead = i + 1 + (WINDOW if i + 1 < n_value else O_WINDOW)
        while started < min(ahead, n_tensor):
            plan[started][0].start()
            started += 1

    for i in range(n_value):
        advance(i)
        if i > 0:
            relay(i - 1)
        if i == V_SUB + 1:
            send_value(3)
    relay(n_value - 1)
    send_value(2)
    send_value(1)

    def piece_range(sub):
        first = n_value + sub * (n - 1)
        return [n_tensor + sub] + list(range(first, first + n - 1))

    def bring(sub, between=None):
        batch = piece_range(sub)
        pass_on(batch[0])
        for at, (before, i) in enumerate(zip(batch, batch[1:])):
            advance(i)
            relay(before)
            if between is not None:
                between(at)

    bring(0)
    value_copies[1].wait_recv()
    value_copies[2].wait_recv()
    total = own_part[...] + part_in[1].astype(jnp.float32) + part_in[2].astype(jnp.float32)
    values = total.astype(jnp.bfloat16)
    for at, (start, head) in enumerate(blocks):
        rows, span = slice(start, start + LEN), slice(head * HEAD_SIZE, (head + 1) * HEAD_SIZE)
        own_context[rows, span] = jnp.dot(
            probs[at], values[rows, span], preferred_element_type=jnp.float32).astype(jnp.bfloat16)

    routes = [(own_context, 2, (other, dp, across)), (own_context, 1, (other, dp, near)),
              (own_context, 0, (other, dp, z)), (context.at[2], 3, (section, dp, near))]
    context_copies = [
        remote(src, context.at[dst], context_send.at[m], context_recv.at[m], to)
        for m, (src, dst, to) in enumerate(routes)]
    for copy in context_copies[:3]:
        copy.start()
    relay(piece_range(0)[-1])
    bring(1)
    context_copies[0].wait_recv()
    context_copies[3].start()
    relay(piece_range(1)[-1])

    out_copies = []

    def chunk(sub, order):
        for i in piece_range(sub):
            if order == 1:
                plan[i][1].wait_recv()
            elif order == 3:
                plan[i][3].wait_recv()
        columns = pl.ds(pl.multiple_of(quarters[order] * quarter + o_start[sub], unit), o_cols[sub])
        total = residual[:, columns].astype(jnp.float32)
        for slot in range(n):
            total = total + jnp.dot(context[slot], wo[slot, :, columns],
                                    preferred_element_type=jnp.float32)
        result[:, columns] = total.astype(jnp.bfloat16)
        copy = pltpu.make_async_copy(result.at[:, columns], out_hbm.at[0, :, columns], out_sem.at[sub, order])
        copy.start()
        out_copies.append(copy)

    for sub in range(2, O_SUB):
        def earlier(at):
            for order in {0: (0, 1), 1: (2, 3)}.get(at, ()):
                chunk(sub - 1, order)
        bring(sub, earlier if sub > 2 else None)
        if sub == 2:
            residual_copy.wait_recv()
            for copy in context_copies[1:]:
                copy.wait_recv()
            for order in range(4):
                chunk(0, order)
        relay(piece_range(sub)[-1])
        if sub == 2:
            for order in range(4):
                chunk(1, order)
    for order in range(4):
        chunk(O_SUB - 1, order)

    for i, piece in enumerate(plan):
        if i not in sent:
            piece[0].wait_send()
        for copy in piece[1:]:
            copy.wait_send()
    for copy in value_copies + context_copies + [residual_copy]:
        copy.wait_send()
    for copy in out_copies:
        copy.wait()


def by_weights(n, inputs, queries, keys, w_value, w_out):
    length, cols = inputs.shape[1:]
    width = w_value.shape[2]
    bf16, dma = jnp.bfloat16, pltpu.SemaphoreType.DMA
    return pl.pallas_call(
        functools.partial(moving_weights, n),
        out_shape=jax.ShapeDtypeStruct(inputs.shape, bf16),
        in_specs=[pl.BlockSpec(memory_space=pl.ANY)] * 5,
        out_specs=pl.BlockSpec(memory_space=pl.ANY),
        scratch_shapes=[
            pltpu.VMEM((length, cols), bf16),
            pltpu.VMEM((length, cols), bf16),
            pltpu.VMEM((length, width), bf16),
            pltpu.VMEM((length, width), bf16),
            pltpu.VMEM((n, cols, width), bf16),
            pltpu.VMEM((n, width, cols), bf16),
            pltpu.VMEM((length // LEN * width // HEAD_SIZE, LEN, LEN), bf16),
            pltpu.VMEM((length, width), jnp.float32),
            pltpu.VMEM((n - 1, length, width), bf16),
            pltpu.VMEM((n - 1, length, width), bf16),
            pltpu.VMEM((length, width), bf16),
            pltpu.VMEM((n, length, width), bf16),
            pltpu.VMEM((length, cols), bf16),
            dma((4,)),
            dma((2,)),
            dma((n - 1, V_SUB, 4)),
            dma((n - 1, V_SUB, 4)),
            dma((n, O_SUB, 4)),
            dma((n, O_SUB, 4)),
            dma((n - 1,)),
            dma((n - 1,)),
            dma((n,)),
            dma((n,)),
            dma((O_SUB, 4)),
        ],
        compiler_params=pltpu.CompilerParams(
            collective_id=0, has_side_effects=True, vmem_limit_bytes=60 * 2**20),
        cost_estimate=pl.CostEstimate(
            flops=4 * length * cols * n * width, bytes_accessed=2 * 4 * n * cols * width,
            transcendentals=length * LEN * width // HEAD_SIZE),
        name="weights_to_activations",
    )(inputs, queries, keys, w_value, w_out)


def by_activations(inputs, queries, keys, w_value, w_out):
    activ = inputs[0]
    weight_v = w_value[0]
    weight_o = w_out[0]
    length = activ.shape[0]
    col_width = activ.shape[1]
    features_all = lax.all_gather(activ, "tensor", axis=1, tiled=True)
    values = jnp.dot(features_all, weight_v, preferred_element_type=jnp.float32)
    values = values.astype(jnp.bfloat16)
    heads_here = weight_v.shape[1] // HEAD_SIZE
    query_rows = queries[0].reshape(length // LEN, LEN, heads_here, HEAD_SIZE)
    key_rows = keys[0].reshape(length // LEN, LEN, heads_here, HEAD_SIZE)
    value_rows = values.reshape(length // LEN, LEN, heads_here, HEAD_SIZE)
    scores = jnp.einsum(
        "bqhd,bkhd->bhqk", query_rows, key_rows, preferred_element_type=jnp.float32
    ) / jnp.sqrt(jnp.float32(HEAD_SIZE))
    rows = lax.broadcasted_iota(jnp.int32, (LEN, LEN), 0)
    cols = lax.broadcasted_iota(jnp.int32, (LEN, LEN), 1)
    scores = jnp.where((cols <= rows)[None, None], scores, jnp.float32(-1e30))
    top = jnp.max(scores, axis=-1, keepdims=True)
    expo = jnp.exp(scores - top)
    probs = (expo / jnp.sum(expo, axis=-1, keepdims=True)).astype(jnp.bfloat16)
    context = jnp.einsum(
        "bhqk,bkhd->bqhd", probs, value_rows, preferred_element_type=jnp.float32
    ).astype(jnp.bfloat16)
    context = context.reshape(length, heads_here * HEAD_SIZE)
    partial_term = jnp.dot(context, weight_o, preferred_element_type=jnp.float32)
    total = lax.psum_scatter(
        partial_term.astype(jnp.bfloat16), "tensor", scatter_dimension=1, tiled=True)
    result = (total.astype(jnp.float32) + activ.astype(jnp.float32)).astype(jnp.bfloat16)
    size = lax.axis_size("section")
    return lax.ppermute(result, "section", [(i, i ^ 1) for i in range(size)])[None]


def solution(mesh):
    n = mesh.shape["tensor"]

    def on_device(inputs, queries, keys, w_value, w_out):
        length, cols = inputs.shape[1:]
        width = w_value.shape[2]
        weights_smaller = n * width <= mesh.shape["dp"] * length
        divides = (cols % (4 * 128 * O_UNITS) == 0 and cols % (4 * 16 * V_SUB) == 0
                   and length % LEN == 0 and n == GROUP and mesh.shape["dp"] == 4)
        if weights_smaller and divides:
            return by_weights(n, inputs, queries, keys, w_value, w_out)
        return by_activations(inputs, queries, keys, w_value, w_out)

    return jax.shard_map(
        on_device,
        mesh=mesh,
        in_specs=(
            P("section", "dp", "tensor"),
            P("section", "dp", "tensor"),
            P("section", "dp", "tensor"),
            P("section", None, "tensor"),
            P("section", "tensor", None),
        ),
        out_specs=P("section", "dp", "tensor"),
        check_vma=False,
    )
```

```python
import functools

import jax
import jax.numpy as jnp
from jax import lax
from jax.experimental import pallas as pl
from jax.experimental.pallas import tpu as pltpu
from jax.sharding import PartitionSpec as P

HEAD_SIZE = 128
LEN = 256
V_SUB = 3
O_SHARES = (2, 2, 1, 1)
O_SUB, O_UNITS = len(O_SHARES), sum(O_SHARES)
WINDOW = 4
FEW = 2
O_WINDOW = 5
GROUP = 4


def flip(index, bit):
    step = 2**bit
    return index + step - 2 * step * lax.rem(index // step, 2)


def flip_by(index, mask):
    for bit in range(mask.bit_length()):
        if mask >> bit & 1:
            index = flip(index, bit)
    return index


def moving_weights(
    n,
    activ_hbm, query_hbm, key_hbm, wv_hbm, wo_hbm, out_hbm,
    activ, residual, query, key, wv, wo, probs, own_part, part_out, part_in, own_context, context, result,
    local_sem, residual_sem, wv_send, wv_recv, wo_send, wo_recv, value_send, value_recv, context_send, context_recv, out_sem,
):
    section = lax.axis_index("section")
    dp = lax.axis_index("dp")
    z = lax.axis_index("tensor")
    length, cols = activ.shape
    quarter = cols // 4
    v_rows = quarter // V_SUB
    unit = quarter // O_UNITS
    o_start = [sum(O_SHARES[:sub]) * unit for sub in range(O_SUB)]
    o_cols = [share * unit for share in O_SHARES]
    core_peer = flip(dp, 0)
    chip_peer = flip(dp, 1)
    diagonal = flip(core_peer, 1)
    quarters = (dp, core_peer, chip_peer, diagonal)
    other = flip(section, 0)

    barrier = pltpu.get_barrier_semaphore()
    for slot in range(1, n):
        pl.semaphore_signal(barrier, inc=1, device_id=(section, dp, flip_by(z, slot)),
                            device_id_type=pl.DeviceIdType.MESH)
    targets = [(section, core_peer, z), (section, chip_peer, z)]
    targets += [(other, dp, flip_by(z, slot)) for slot in range(n)]
    for target in targets:
        pl.semaphore_signal(barrier, inc=1, device_id=target, device_id_type=pl.DeviceIdType.MESH)

    def remote(src, dst, send, recv, target):
        return pltpu.make_async_remote_copy(
            src_ref=src, dst_ref=dst, send_sem=send, recv_sem=recv,
            device_id=target, device_id_type=pl.DeviceIdType.MESH)

    own = pl.multiple_of(z * cols, cols)
    locals_ = [
        pltpu.make_async_copy(activ_hbm.at[0], activ, local_sem.at[0]),
        pltpu.make_async_copy(query_hbm.at[0], query, local_sem.at[1]),
        pltpu.make_async_copy(key_hbm.at[0], key, local_sem.at[2]),
        pltpu.make_async_copy(wv_hbm.at[0, pl.ds(own, cols), :], wv.at[0], local_sem.at[3]),
    ]
    pl.semaphore_wait(barrier, 2 * n + 1)

    pieces = [("v", 3, sub) for sub in range(V_SUB)]
    pieces += [("v", slot, sub) for sub in range(V_SUB) for slot in (2, 1)]
    n_value = len(pieces)
    pieces += [("o", slot, sub) for sub in range(O_SUB) for slot in (3, 2, 1)]
    pieces += [("o", 0, sub) for sub in range(O_SUB)]
    n_tensor = n_value + O_SUB * (n - 1)

    def v_at(slot, which, sub):
        rows = pl.ds(pl.multiple_of(which * quarter + sub * v_rows, v_rows), v_rows)
        return wv.at[slot, rows, :]

    def o_at(slot, which, sub):
        columns = pl.ds(pl.multiple_of(which * quarter + o_start[sub], unit), o_cols[sub])
        return wo.at[slot, :, columns]

    def copies(piece):
        kind, slot, sub = piece
        peer = flip_by(z, slot)
        if kind == "v":
            start = pl.multiple_of(peer * cols + dp * quarter + sub * v_rows, v_rows)
            source = wv_hbm.at[0, pl.ds(start, v_rows), :]
            at, send, recv, index, target = v_at, wv_send, wv_recv, slot - 1, (section, dp, peer)
        else:
            start = pl.multiple_of(peer * cols + dp * quarter + o_start[sub], unit)
            source = wo_hbm.at[0, :, pl.ds(start, o_cols[sub])]
            at, send, recv, index, target = o_at, wo_send, wo_recv, slot, (other, dp, peer)
        mine, far = at(slot, dp, sub), at(slot, chip_peer, sub)
        def sems(hop):
            return send.at[index, sub, hop], recv.at[index, sub, hop]
        return (
            remote(source, mine, *sems(0), target),
            remote(mine, mine, *sems(1), (section, core_peer, z)),
            remote(mine, mine, *sems(2), (section, chip_peer, z)),
            remote(far, far, *sems(3), (section, core_peer, z)),
        )

    plan = [copies(piece) for piece in pieces]
    for i in range(WINDOW):
        plan[i][0].start()
    for copy in locals_:
        copy.start()
    residual_copy = remote(activ_hbm.at[0], residual, residual_sem.at[0], residual_sem.at[1], (other, dp, z))
    for i in range(n_tensor, len(plan)):
        plan[i][0].start()
    residual_copy.start()

    def pass_on(i):
        plan[i][0].wait_recv()
        plan[i][2].start()
        plan[i][1].start()

    def relay(i):
        plan[i][2].wait_recv()
        plan[i][3].start()

    locals_[1].wait()
    locals_[2].wait()
    causal = lax.broadcasted_iota(jnp.int32, (LEN, LEN), 1) <= lax.broadcasted_iota(jnp.int32, (LEN, LEN), 0)
    scale = 1.0 / HEAD_SIZE**0.5
    heads = query.shape[1] // HEAD_SIZE
    blocks = [(start, head) for start in range(0, length, LEN) for head in range(heads)]
    for at, (start, head) in enumerate(blocks):
        rows, span = slice(start, start + LEN), slice(head * HEAD_SIZE, (head + 1) * HEAD_SIZE)
        scores = lax.dot_general(query[rows, span], key[rows, span], (((1,), (1,)), ((), ())),
                                 preferred_element_type=jnp.float32) * scale
        scores = jnp.where(causal, scores, -1e30)
        expo = jnp.exp(scores - jnp.max(scores, axis=-1, keepdims=True))
        probs[at] = (expo / jnp.sum(expo, axis=-1, keepdims=True)).astype(jnp.bfloat16)
    locals_[0].wait()
    locals_[3].wait()
    own_part[...] = jnp.dot(activ[...], wv[0], preferred_element_type=jnp.float32)

    near, across = flip_by(z, 1), flip_by(z, 2)
    value_copies = [
        remote(part_out.at[m], part_in.at[m], value_send.at[m], value_recv.at[m], (section, dp, to))
        for m, to in enumerate((near, across, near))]

    def send_value(slot):
        for i, (kind, at, _) in enumerate(pieces):
            if kind == "v" and at == slot:
                plan[i][1].wait_recv()
                plan[i][3].wait_recv()
        term = jnp.dot(activ[...], wv[slot], preferred_element_type=jnp.float32)
        if slot == 2:
            value_copies[0].wait_recv()
            term = term + part_in[0].astype(jnp.float32)
        part_out[3 - slot] = term.astype(jnp.bfloat16)
        value_copies[3 - slot].start()

    started = WINDOW
    sent = set()

    def start_until(end):
        nonlocal started
        while started < min(end, n_tensor):
            plan[started][0].start()
            started += 1

    def advance(i, ahead):
        pass_on(i)
        if started < n_tensor:
            plan[i][0].wait_send()
            sent.add(i)
        start_until(i + 1 + ahead)

    for i in range(n_value):
        advance(i, min(WINDOW, n_value + FEW - i - 1))
        if i > 0:
            relay(i - 1)
        if i == V_SUB + 1:
            send_value(3)
    relay(n_value - 1)
    send_value(2)
    send_value(1)

    def piece_range(sub):
        first = n_value + sub * (n - 1)
        return [n_tensor + sub] + list(range(first, first + n - 1))

    def bring(sub, ahead, between=None):
        batch = piece_range(sub)
        pass_on(batch[0])
        for at, (before, i) in enumerate(zip(batch, batch[1:])):
            advance(i, ahead)
            relay(before)
            if between is not None:
                between(at)

    bring(0, FEW)
    value_copies[1].wait_recv()
    value_copies[2].wait_recv()
    total = own_part[...] + part_in[1].astype(jnp.float32) + part_in[2].astype(jnp.float32)
    values = total.astype(jnp.bfloat16)
    for at, (start, head) in enumerate(blocks):
        rows, span = slice(start, start + LEN), slice(head * HEAD_SIZE, (head + 1) * HEAD_SIZE)
        own_context[rows, span] = jnp.dot(
            probs[at], values[rows, span], preferred_element_type=jnp.float32).astype(jnp.bfloat16)

    routes = [(own_context, 2, (other, dp, across)), (own_context, 1, (other, dp, near)),
              (own_context, 0, (other, dp, z)), (context.at[2], 3, (section, dp, near))]
    context_copies = [
        remote(src, context.at[dst], context_send.at[m], context_recv.at[m], to)
        for m, (src, dst, to) in enumerate(routes)]
    for copy in context_copies[:3]:
        copy.start()
    start_until(n_value + n - 1 + O_WINDOW)
    relay(piece_range(0)[-1])
    context_copies[0].wait_recv()
    context_copies[3].start()
    bring(1, O_WINDOW)
    relay(piece_range(1)[-1])

    out_copies = []

    def chunk(sub, order):
        for i in piece_range(sub):
            if order == 1:
                plan[i][1].wait_recv()
            elif order == 3:
                plan[i][3].wait_recv()
        columns = pl.ds(pl.multiple_of(quarters[order] * quarter + o_start[sub], unit), o_cols[sub])
        total = residual[:, columns].astype(jnp.float32)
        for slot in range(n):
            total = total + jnp.dot(context[slot], wo[slot, :, columns],
                                    preferred_element_type=jnp.float32)
        result[:, columns] = total.astype(jnp.bfloat16)
        copy = pltpu.make_async_copy(result.at[:, columns], out_hbm.at[0, :, columns], out_sem.at[sub, order])
        copy.start()
        out_copies.append(copy)

    for sub in range(2, O_SUB):
        def earlier(at):
            for order in {0: (0, 1), 1: (2, 3)}.get(at, ()):
                chunk(sub - 1, order)
        bring(sub, O_WINDOW, earlier if sub > 2 else None)
        if sub == 2:
            residual_copy.wait_recv()
            for copy in context_copies[1:]:
                copy.wait_recv()
            for order in range(4):
                chunk(0, order)
        relay(piece_range(sub)[-1])
        if sub == 2:
            for order in range(4):
                chunk(1, order)
    for order in range(4):
        chunk(O_SUB - 1, order)

    for i, piece in enumerate(plan):
        if i not in sent:
            piece[0].wait_send()
        for copy in piece[1:]:
            copy.wait_send()
    for copy in value_copies + context_copies + [residual_copy]:
        copy.wait_send()
    for copy in out_copies:
        copy.wait()


def by_weights(n, inputs, queries, keys, w_value, w_out):
    length, cols = inputs.shape[1:]
    width = w_value.shape[2]
    bf16, dma = jnp.bfloat16, pltpu.SemaphoreType.DMA
    return pl.pallas_call(
        functools.partial(moving_weights, n),
        out_shape=jax.ShapeDtypeStruct(inputs.shape, bf16),
        in_specs=[pl.BlockSpec(memory_space=pl.ANY)] * 5,
        out_specs=pl.BlockSpec(memory_space=pl.ANY),
        scratch_shapes=[
            pltpu.VMEM((length, cols), bf16),
            pltpu.VMEM((length, cols), bf16),
            pltpu.VMEM((length, width), bf16),
            pltpu.VMEM((length, width), bf16),
            pltpu.VMEM((n, cols, width), bf16),
            pltpu.VMEM((n, width, cols), bf16),
            pltpu.VMEM((length // LEN * width // HEAD_SIZE, LEN, LEN), bf16),
            pltpu.VMEM((length, width), jnp.float32),
            pltpu.VMEM((n - 1, length, width), bf16),
            pltpu.VMEM((n - 1, length, width), bf16),
            pltpu.VMEM((length, width), bf16),
            pltpu.VMEM((n, length, width), bf16),
            pltpu.VMEM((length, cols), bf16),
            dma((4,)),
            dma((2,)),
            dma((n - 1, V_SUB, 4)),
            dma((n - 1, V_SUB, 4)),
            dma((n, O_SUB, 4)),
            dma((n, O_SUB, 4)),
            dma((n - 1,)),
            dma((n - 1,)),
            dma((n,)),
            dma((n,)),
            dma((O_SUB, 4)),
        ],
        compiler_params=pltpu.CompilerParams(
            collective_id=0, has_side_effects=True, vmem_limit_bytes=60 * 2**20),
        cost_estimate=pl.CostEstimate(
            flops=4 * length * cols * n * width, bytes_accessed=2 * 4 * n * cols * width,
            transcendentals=length * LEN * width // HEAD_SIZE),
        name="weights_to_activations",
    )(inputs, queries, keys, w_value, w_out)


def by_activations(inputs, queries, keys, w_value, w_out):
    activ = inputs[0]
    weight_v = w_value[0]
    weight_o = w_out[0]
    length = activ.shape[0]
    col_width = activ.shape[1]
    features_all = lax.all_gather(activ, "tensor", axis=1, tiled=True)
    values = jnp.dot(features_all, weight_v, preferred_element_type=jnp.float32)
    values = values.astype(jnp.bfloat16)
    heads_here = weight_v.shape[1] // HEAD_SIZE
    query_rows = queries[0].reshape(length // LEN, LEN, heads_here, HEAD_SIZE)
    key_rows = keys[0].reshape(length // LEN, LEN, heads_here, HEAD_SIZE)
    value_rows = values.reshape(length // LEN, LEN, heads_here, HEAD_SIZE)
    scores = jnp.einsum(
        "bqhd,bkhd->bhqk", query_rows, key_rows, preferred_element_type=jnp.float32
    ) / jnp.sqrt(jnp.float32(HEAD_SIZE))
    rows = lax.broadcasted_iota(jnp.int32, (LEN, LEN), 0)
    cols = lax.broadcasted_iota(jnp.int32, (LEN, LEN), 1)
    scores = jnp.where((cols <= rows)[None, None], scores, jnp.float32(-1e30))
    top = jnp.max(scores, axis=-1, keepdims=True)
    expo = jnp.exp(scores - top)
    probs = (expo / jnp.sum(expo, axis=-1, keepdims=True)).astype(jnp.bfloat16)
    context = jnp.einsum(
        "bhqk,bkhd->bqhd", probs, value_rows, preferred_element_type=jnp.float32
    ).astype(jnp.bfloat16)
    context = context.reshape(length, heads_here * HEAD_SIZE)
    partial_term = jnp.dot(context, weight_o, preferred_element_type=jnp.float32)
    total = lax.psum_scatter(
        partial_term.astype(jnp.bfloat16), "tensor", scatter_dimension=1, tiled=True)
    result = (total.astype(jnp.float32) + activ.astype(jnp.float32)).astype(jnp.bfloat16)
    size = lax.axis_size("section")
    return lax.ppermute(result, "section", [(i, i ^ 1) for i in range(size)])[None]


def solution(mesh):
    n = mesh.shape["tensor"]

    def on_device(inputs, queries, keys, w_value, w_out):
        length, cols = inputs.shape[1:]
        width = w_value.shape[2]
        weights_smaller = n * width <= mesh.shape["dp"] * length
        divides = (cols % (4 * 128 * O_UNITS) == 0 and cols % (4 * 16 * V_SUB) == 0
                   and length % LEN == 0 and n == GROUP and mesh.shape["dp"] == 4)
        if weights_smaller and divides:
            return by_weights(n, inputs, queries, keys, w_value, w_out)
        return by_activations(inputs, queries, keys, w_value, w_out)

    return jax.shard_map(
        on_device,
        mesh=mesh,
        in_specs=(
            P("section", "dp", "tensor"),
            P("section", "dp", "tensor"),
            P("section", "dp", "tensor"),
            P("section", None, "tensor"),
            P("section", "tensor", None),
        ),
        out_specs=P("section", "dp", "tensor"),
        check_vma=False,
    )
```

```python
import functools

import jax
import jax.numpy as jnp
from jax import lax
from jax.experimental import pallas as pl
from jax.experimental.pallas import tpu as pltpu
from jax.sharding import PartitionSpec as P

HEAD_SIZE = 128
LEN = 256
V_SUB = 3
O_SHARES = (2, 2, 1, 1)
O_SUB, O_UNITS = len(O_SHARES), sum(O_SHARES)
WINDOW = 4
GROUP = 4


def flip(index, bit):
    step = 2**bit
    return index + step - 2 * step * lax.rem(index // step, 2)


def flip_by(index, mask):
    for bit in range(mask.bit_length()):
        if mask >> bit & 1:
            index = flip(index, bit)
    return index


def moving_weights(
    n,
    activ_hbm, query_hbm, key_hbm, wv_hbm, wo_hbm, out_hbm,
    activ, residual, query, key, wv, wo, probs, own_part, part_out, part_in, own_context, context, result,
    local_sem, residual_sem, wv_send, wv_recv, wo_send, wo_recv, value_send, value_recv, context_send, context_recv, out_sem,
):
    section = lax.axis_index("section")
    dp = lax.axis_index("dp")
    z = lax.axis_index("tensor")
    length, cols = activ.shape
    quarter = cols // 4
    v_rows = quarter // V_SUB
    unit = quarter // O_UNITS
    o_start = [sum(O_SHARES[:sub]) * unit for sub in range(O_SUB)]
    o_cols = [share * unit for share in O_SHARES]
    core_peer = flip(dp, 0)
    chip_peer = flip(dp, 1)
    diagonal = flip(core_peer, 1)
    quarters = (dp, core_peer, chip_peer, diagonal)
    other = flip(section, 0)

    barrier = pltpu.get_barrier_semaphore()
    for slot in range(1, n):
        pl.semaphore_signal(barrier, inc=1, device_id=(section, dp, flip_by(z, slot)),
                            device_id_type=pl.DeviceIdType.MESH)
    targets = [(section, core_peer, z), (section, chip_peer, z)]
    targets += [(other, dp, flip_by(z, slot)) for slot in range(n)]
    for target in targets:
        pl.semaphore_signal(barrier, inc=1, device_id=target, device_id_type=pl.DeviceIdType.MESH)

    def remote(src, dst, send, recv, target):
        return pltpu.make_async_remote_copy(
            src_ref=src, dst_ref=dst, send_sem=send, recv_sem=recv,
            device_id=target, device_id_type=pl.DeviceIdType.MESH)

    own = pl.multiple_of(z * cols, cols)
    locals_ = [
        pltpu.make_async_copy(activ_hbm.at[0], activ, local_sem.at[0]),
        pltpu.make_async_copy(query_hbm.at[0], query, local_sem.at[1]),
        pltpu.make_async_copy(key_hbm.at[0], key, local_sem.at[2]),
        pltpu.make_async_copy(wv_hbm.at[0, pl.ds(own, cols), :], wv.at[0], local_sem.at[3]),
    ]
    for copy in locals_:
        copy.start()
    pl.semaphore_wait(barrier, 2 * n + 1)

    pieces = [("v", 3, sub) for sub in range(V_SUB)]
    pieces += [("v", slot, sub) for sub in range(V_SUB) for slot in (2, 1)]
    n_value = len(pieces)
    pieces += [("o", slot, sub) for sub in range(O_SUB) for slot in (3, 2, 1)]
    pieces += [("o", 0, sub) for sub in range(O_SUB)]
    n_tensor = n_value + O_SUB * (n - 1)

    def v_at(slot, which, sub):
        rows = pl.ds(pl.multiple_of(which * quarter + sub * v_rows, v_rows), v_rows)
        return wv.at[slot, rows, :]

    def o_at(slot, which, sub):
        columns = pl.ds(pl.multiple_of(which * quarter + o_start[sub], unit), o_cols[sub])
        return wo.at[slot, :, columns]

    def copies(piece):
        kind, slot, sub = piece
        peer = flip_by(z, slot)
        if kind == "v":
            start = pl.multiple_of(peer * cols + dp * quarter + sub * v_rows, v_rows)
            source = wv_hbm.at[0, pl.ds(start, v_rows), :]
            at, send, recv, index, target = v_at, wv_send, wv_recv, slot - 1, (section, dp, peer)
        else:
            start = pl.multiple_of(peer * cols + dp * quarter + o_start[sub], unit)
            source = wo_hbm.at[0, :, pl.ds(start, o_cols[sub])]
            at, send, recv, index, target = o_at, wo_send, wo_recv, slot, (other, dp, peer)
        mine, far = at(slot, dp, sub), at(slot, chip_peer, sub)
        def sems(hop):
            return send.at[index, sub, hop], recv.at[index, sub, hop]
        return (
            remote(source, mine, *sems(0), target),
            remote(mine, mine, *sems(1), (section, core_peer, z)),
            remote(mine, mine, *sems(2), (section, chip_peer, z)),
            remote(far, far, *sems(3), (section, core_peer, z)),
        )

    plan = [copies(piece) for piece in pieces]
    for i in range(WINDOW):
        plan[i][0].start()
    residual_copy = remote(activ_hbm.at[0], residual, residual_sem.at[0], residual_sem.at[1], (other, dp, z))
    for i in range(n_tensor, len(plan)):
        plan[i][0].start()
    residual_copy.start()

    def pass_on(i):
        plan[i][0].wait_recv()
        plan[i][2].start()
        plan[i][1].start()

    def relay(i):
        plan[i][2].wait_recv()
        plan[i][3].start()

    locals_[1].wait()
    locals_[2].wait()
    causal = lax.broadcasted_iota(jnp.int32, (LEN, LEN), 1) <= lax.broadcasted_iota(jnp.int32, (LEN, LEN), 0)
    scale = 1.0 / HEAD_SIZE**0.5
    heads = query.shape[1] // HEAD_SIZE
    blocks = [(start, head) for start in range(0, length, LEN) for head in range(heads)]
    for at, (start, head) in enumerate(blocks):
        rows, span = slice(start, start + LEN), slice(head * HEAD_SIZE, (head + 1) * HEAD_SIZE)
        scores = lax.dot_general(query[rows, span], key[rows, span], (((1,), (1,)), ((), ())),
                                 preferred_element_type=jnp.float32) * scale
        scores = jnp.where(causal, scores, -1e30)
        expo = jnp.exp(scores - jnp.max(scores, axis=-1, keepdims=True))
        probs[at] = (expo / jnp.sum(expo, axis=-1, keepdims=True)).astype(jnp.bfloat16)
    locals_[0].wait()
    locals_[3].wait()
    own_part[...] = jnp.dot(activ[...], wv[0], preferred_element_type=jnp.float32)

    near, across = flip_by(z, 1), flip_by(z, 2)
    value_copies = [
        remote(part_out.at[m], part_in.at[m], value_send.at[m], value_recv.at[m], (section, dp, to))
        for m, to in enumerate((near, across, near))]

    def send_value(slot):
        for i, (kind, at, _) in enumerate(pieces):
            if kind == "v" and at == slot:
                plan[i][1].wait_recv()
                plan[i][3].wait_recv()
        term = jnp.dot(activ[...], wv[slot], preferred_element_type=jnp.float32)
        if slot == 2:
            value_copies[0].wait_recv()
            term = term + part_in[0].astype(jnp.float32)
        part_out[3 - slot] = term.astype(jnp.bfloat16)
        value_copies[3 - slot].start()

    def advance(i):
        pass_on(i)
        if i + WINDOW < n_tensor:
            plan[i][0].wait_send()
            plan[i + WINDOW][0].start()

    for i in range(n_value):
        advance(i)
        if i > 0:
            relay(i - 1)
        if i == V_SUB + 1:
            send_value(3)
    relay(n_value - 1)
    send_value(2)
    send_value(1)

    def piece_range(sub):
        first = n_value + sub * (n - 1)
        return [n_tensor + sub] + list(range(first, first + n - 1))

    def bring(sub, between=None):
        batch = piece_range(sub)
        pass_on(batch[0])
        for before, i in zip(batch, batch[1:]):
            advance(i)
            relay(before)
            if between is not None and i == batch[1]:
                between()

    bring(0)
    value_copies[1].wait_recv()
    value_copies[2].wait_recv()
    total = own_part[...] + part_in[1].astype(jnp.float32) + part_in[2].astype(jnp.float32)
    values = total.astype(jnp.bfloat16)
    for at, (start, head) in enumerate(blocks):
        rows, span = slice(start, start + LEN), slice(head * HEAD_SIZE, (head + 1) * HEAD_SIZE)
        own_context[rows, span] = jnp.dot(
            probs[at], values[rows, span], preferred_element_type=jnp.float32).astype(jnp.bfloat16)

    routes = [(own_context, 2, (other, dp, across)), (own_context, 1, (other, dp, near)),
              (own_context, 0, (other, dp, z)), (context.at[2], 3, (section, dp, near))]
    context_copies = [
        remote(src, context.at[dst], context_send.at[m], context_recv.at[m], to)
        for m, (src, dst, to) in enumerate(routes)]
    for copy in context_copies[:3]:
        copy.start()
    relay(piece_range(0)[-1])
    bring(1)
    context_copies[0].wait_recv()
    context_copies[3].start()
    relay(piece_range(1)[-1])

    out_copies = []

    def chunk(sub, order):
        for i in piece_range(sub):
            if order == 1:
                plan[i][1].wait_recv()
            elif order == 3:
                plan[i][3].wait_recv()
        columns = pl.ds(pl.multiple_of(quarters[order] * quarter + o_start[sub], unit), o_cols[sub])
        total = residual[:, columns].astype(jnp.float32)
        for slot in range(n):
            total = total + jnp.dot(context[slot], wo[slot, :, columns],
                                    preferred_element_type=jnp.float32)
        result[:, columns] = total.astype(jnp.bfloat16)
        copy = pltpu.make_async_copy(result.at[:, columns], out_hbm.at[0, :, columns], out_sem.at[sub, order])
        copy.start()
        out_copies.append(copy)

    for sub in range(2, O_SUB):
        def earlier():
            for order in range(4):
                chunk(sub - 1, order)
        bring(sub, earlier if sub > 2 else None)
        if sub == 2:
            residual_copy.wait_recv()
            for copy in context_copies[1:]:
                copy.wait_recv()
            for order in range(4):
                chunk(0, order)
        relay(piece_range(sub)[-1])
        if sub == 2:
            for order in range(4):
                chunk(1, order)
    for order in range(4):
        chunk(O_SUB - 1, order)

    for i, piece in enumerate(plan):
        if not i + WINDOW < n_tensor:
            piece[0].wait_send()
        for copy in piece[1:]:
            copy.wait_send()
    for copy in value_copies + context_copies + [residual_copy]:
        copy.wait_send()
    for copy in out_copies:
        copy.wait()


def by_weights(n, inputs, queries, keys, w_value, w_out):
    length, cols = inputs.shape[1:]
    width = w_value.shape[2]
    bf16, dma = jnp.bfloat16, pltpu.SemaphoreType.DMA
    return pl.pallas_call(
        functools.partial(moving_weights, n),
        out_shape=jax.ShapeDtypeStruct(inputs.shape, bf16),
        in_specs=[pl.BlockSpec(memory_space=pl.ANY)] * 5,
        out_specs=pl.BlockSpec(memory_space=pl.ANY),
        scratch_shapes=[
            pltpu.VMEM((length, cols), bf16),
            pltpu.VMEM((length, cols), bf16),
            pltpu.VMEM((length, width), bf16),
            pltpu.VMEM((length, width), bf16),
            pltpu.VMEM((n, cols, width), bf16),
            pltpu.VMEM((n, width, cols), bf16),
            pltpu.VMEM((length // LEN * width // HEAD_SIZE, LEN, LEN), bf16),
            pltpu.VMEM((length, width), jnp.float32),
            pltpu.VMEM((n - 1, length, width), bf16),
            pltpu.VMEM((n - 1, length, width), bf16),
            pltpu.VMEM((length, width), bf16),
            pltpu.VMEM((n, length, width), bf16),
            pltpu.VMEM((length, cols), bf16),
            dma((4,)),
            dma((2,)),
            dma((n - 1, V_SUB, 4)),
            dma((n - 1, V_SUB, 4)),
            dma((n, O_SUB, 4)),
            dma((n, O_SUB, 4)),
            dma((n - 1,)),
            dma((n - 1,)),
            dma((n,)),
            dma((n,)),
            dma((O_SUB, 4)),
        ],
        compiler_params=pltpu.CompilerParams(
            collective_id=0, has_side_effects=True, vmem_limit_bytes=60 * 2**20),
        cost_estimate=pl.CostEstimate(
            flops=4 * length * cols * n * width, bytes_accessed=2 * 4 * n * cols * width,
            transcendentals=length * LEN * width // HEAD_SIZE),
        name="weights_to_activations",
    )(inputs, queries, keys, w_value, w_out)


def by_activations(inputs, queries, keys, w_value, w_out):
    activ = inputs[0]
    weight_v = w_value[0]
    weight_o = w_out[0]
    length = activ.shape[0]
    col_width = activ.shape[1]
    features_all = lax.all_gather(activ, "tensor", axis=1, tiled=True)
    values = jnp.dot(features_all, weight_v, preferred_element_type=jnp.float32)
    values = values.astype(jnp.bfloat16)
    heads_here = weight_v.shape[1] // HEAD_SIZE
    query_rows = queries[0].reshape(length // LEN, LEN, heads_here, HEAD_SIZE)
    key_rows = keys[0].reshape(length // LEN, LEN, heads_here, HEAD_SIZE)
    value_rows = values.reshape(length // LEN, LEN, heads_here, HEAD_SIZE)
    scores = jnp.einsum(
        "bqhd,bkhd->bhqk", query_rows, key_rows, preferred_element_type=jnp.float32
    ) / jnp.sqrt(jnp.float32(HEAD_SIZE))
    rows = lax.broadcasted_iota(jnp.int32, (LEN, LEN), 0)
    cols = lax.broadcasted_iota(jnp.int32, (LEN, LEN), 1)
    scores = jnp.where((cols <= rows)[None, None], scores, jnp.float32(-1e30))
    top = jnp.max(scores, axis=-1, keepdims=True)
    expo = jnp.exp(scores - top)
    probs = (expo / jnp.sum(expo, axis=-1, keepdims=True)).astype(jnp.bfloat16)
    context = jnp.einsum(
        "bhqk,bkhd->bqhd", probs, value_rows, preferred_element_type=jnp.float32
    ).astype(jnp.bfloat16)
    context = context.reshape(length, heads_here * HEAD_SIZE)
    partial_term = jnp.dot(context, weight_o, preferred_element_type=jnp.float32)
    total = lax.psum_scatter(
        partial_term.astype(jnp.bfloat16), "tensor", scatter_dimension=1, tiled=True)
    result = (total.astype(jnp.float32) + activ.astype(jnp.float32)).astype(jnp.bfloat16)
    size = lax.axis_size("section")
    return lax.ppermute(result, "section", [(i, i ^ 1) for i in range(size)])[None]


def solution(mesh):
    n = mesh.shape["tensor"]

    def on_device(inputs, queries, keys, w_value, w_out):
        length, cols = inputs.shape[1:]
        width = w_value.shape[2]
        weights_smaller = n * width <= mesh.shape["dp"] * length
        divides = (cols % (4 * 128 * O_UNITS) == 0 and cols % (4 * 16 * V_SUB) == 0
                   and length % LEN == 0 and n == GROUP and mesh.shape["dp"] == 4)
        if weights_smaller and divides:
            return by_weights(n, inputs, queries, keys, w_value, w_out)
        return by_activations(inputs, queries, keys, w_value, w_out)

    return jax.shard_map(
        on_device,
        mesh=mesh,
        in_specs=(
            P("section", "dp", "tensor"),
            P("section", "dp", "tensor"),
            P("section", "dp", "tensor"),
            P("section", None, "tensor"),
            P("section", "tensor", None),
        ),
        out_specs=P("section", "dp", "tensor"),
        check_vma=False,
    )
```
